256 devices in a mesh: gx: 8 (over z_hi, core), gy: 4 (over y), gz: 8 (over z_lo, x).
Axes of the slice: x: 4, y: 4, z: 8 (z_hi: 4, z_lo: 2; z = z_hi * 2 + z_lo), core: 2. Of those that a mesh axis runs over, the one named last changes fastest.
Arguments:
- pressure_now: float32 [128, 256, 1024], P('gx', 'gy', 'gz'), may hold values from -6 to 6
- pressure_prev: float32 [128, 256, 1024], P('gx', 'gy', 'gz'), may hold values from -6 to 6
- boundary_mask: int32 [128, 256, 1024], P('gx', 'gy', 'gz'), may hold values 0 or 1
- writer: int32 [8, 4], P('gx', 'gy'), may hold values from 0 to 7
Outputs:
- pressure: float32 [128, 256, 1024], P('gx', 'gy', 'gz')
- collected: float32 [8, 64, 128, 512], P('gz', 'gx', 'gy')
The draws below stay inside these ranges and needn't reach their ends.
All inputs are finite; a program needn't handle non-finite values. No bound on the sum of `boundary_mask` on one device may be relied on, other than what follows from the above.
Results may differ from the reference program's by a relative error of at most 0.00017.
Values sent between devices are 32-bit elements; how exact they have to be, the bound alone decides.
No kernel may reach another device: no remote copies, remote signals or barrier semaphores. Data moves between devices by JAX's collectives and lax.ppermute only.
A program may use at most 64 MiB of HBM per device.

```python
import jax
import jax.numpy as jnp
from jax import lax

CX = 16
CY = 64
ITERS = 4
NX = 128
NY = 256
NZ = 1024
N_GX = 8
N_GY = 4
N_GZ = 8


def plant(drawn, own_key, least, top_value):
    longest = drawn.shape.index(max(drawn.shape))
    spots = []
    for shift in (0, 1):
        where = [jax.random.randint(jax.random.fold_in(own_key, axis), (), 0, length) for axis, length in enumerate(drawn.shape)]
        where[longest] = (where[longest] + shift) % drawn.shape[longest]
        spots.append(tuple(where))
    return drawn.at[spots[0]].set(least).at[spots[1]].set(top_value)


def shard_levels(key, shape, cuts, low, top_value):
    factor_of, own = 1.0, jax.random.fold_in(key, 6)
    for dim, parts in cuts:
        steps = jnp.exp(jax.random.uniform(jax.random.fold_in(own, dim), (parts,), jnp.float32, low / len(cuts), top_value / len(cuts)))
        factor_of = factor_of * jnp.repeat(steps, shape[dim] // parts).reshape([-1 if axis == dim else 1 for axis in range(len(shape))])
    return factor_of


def scatter_about(rng, extent, spread, limit, pieces=(), held_as=jnp.bfloat16):
    array = spread * jax.random.normal(rng, extent, jnp.float32)
    if pieces:
        array = array * shard_levels(rng, extent, pieces, -0.22, 0.18)
    return jnp.clip(array, -limit, limit).astype(held_as)


def setup_inputs(seed: int = 0) -> dict:
    keys = jax.random.split(jax.random.key(seed), 5)
    return {
        "pressure_now": scatter_about(keys[0], (NX, NY, NZ), 1.0, 6.0, ((0, 8), (1, 4), (2, 8)), jnp.float32),
        "pressure_prev": scatter_about(keys[1], (NX, NY, NZ), 1.0, 6.0, ((0, 8), (1, 4), (2, 8)), jnp.float32),
        "boundary_mask": plant((jax.random.randint(keys[2], (NX, NY, NZ), 0, 4) < 1).astype(jnp.int32), jax.random.fold_in(keys[2], 1), 0, 1),
        "writer": plant(jax.random.randint(keys[3], (N_GX, N_GY), 0, N_GZ), jax.random.fold_in(keys[3], 1), 0, N_GZ - 1).astype(jnp.int32),
    }


def brick_matrix(length):
    rows = jnp.arange(length)[:, None]
    cols = jnp.arange(length // 2)[None, :]
    freq = (cols % 4).astype(jnp.float32)
    place = (rows % 8).astype(jnp.float32)
    scale = jnp.where(cols % 4 == 0, jnp.sqrt(jnp.float32(1.0 / 8.0)), jnp.sqrt(jnp.float32(2.0 / 8.0)))
    values = scale * jnp.cos(jnp.float32(jnp.pi) * (2.0 * place + 1.0) * freq / 16.0)
    return jnp.where(rows // 8 == cols // 4, values, jnp.float32(0.0)).astype(jnp.float32)

def neighbours(padded):
    total = padded[2:, 1:-1, 1:-1] + padded[:-2, 1:-1, 1:-1]
    total = total + padded[1:-1, 2:, 1:-1] + padded[1:-1, :-2, 1:-1]
    total = total + padded[1:-1, 1:-1, 2:] + padded[1:-1, 1:-1, :-2]
    return total

def reference(pressure_now, pressure_prev, boundary_mask, writer):
    weights = boundary_mask.astype(jnp.float32)
    current, previous = (pressure_now, pressure_prev)
    for turn_index in range(ITERS):
        padded = jnp.pad(current, 1)
        following = (neighbours(padded) / 3.0 - previous) * (1.0 - 0.5 * weights)
        previous = current
        current = following
    kernel = brick_matrix(8).T
    size_x, size_y, size_z = current.shape
    bricks = current.reshape(size_x // 8, 8, size_y // 8, 8, size_z // 8, 8)
    coef = jnp.einsum('ai,bj,ck,xiyjzk->xaybzc', kernel, kernel, kernel, bricks, precision=lax.Precision.HIGHEST)
    coef = coef.reshape(size_x // 2, size_y // 2, size_z // 2)
    owners = jnp.repeat(jnp.repeat(writer, CX // 2, axis=0), CY // 2, axis=1)
    slots = jnp.arange(N_GZ).astype(jnp.int32)
    chosen = owners[None, :, :, None] == slots[:, None, None, None]
    collected = jnp.where(chosen, coef[None], jnp.float32(0.0))
    return (current, collected)
```

```python
import functools

import jax
import jax.numpy as jnp
import numpy as np
from jax import lax
from jax.experimental import pallas as pl
from jax.experimental.pallas import tpu as pltpu
from jax.sharding import PartitionSpec as P

ITERS = 4
X, Y, Z = 16, 64, 128
W = ITERS
N_FACE = W + 2 * (W - 1)
F32 = jnp.float32


def swap_a(n):
    return [(i, i ^ 1) for i in range(n)]


def swap_b(n):
    return [(i, (i + 1) % n if i % 2 else (i - 1) % n) for i in range(n)]


def dct_rows():
    k = np.arange(4)[:, None]
    i = np.arange(8)[None, :]
    scale = np.where(k == 0, np.sqrt(1.0 / 8.0), np.sqrt(2.0 / 8.0))
    return scale * np.cos(np.pi * (2 * i + 1) * k / 16.0)


def is_even(axis):
    return lax.rem(lax.axis_index(axis), 2) == 0


def b_is_inside(axis):
    index, count = lax.axis_index(axis), lax.axis_size(axis)
    return jnp.logical_and(index > 0, index < count - 1)


def iota(shape, dim):
    return lax.broadcasted_iota(jnp.int32, shape, dim)


def gain_of(mask):
    return 1.0 - 0.5 * mask.astype(F32)


def load(p, q, m, arr, x, rows=slice(None)):
    if arr == 0:
        return p[x, rows, :]
    if arr == 1:
        return q[x, rows, :]
    return gain_of(m[x, rows, :])


def y_pairs():
    return [((0, x), (1, x)) for x in range(X)] + [((2, 2 * i), (2, 2 * i + 1)) for i in range(X // 2)]


def face(p, q, m, right, store):
    p0 = jnp.where(right, X - W, 0)
    q0 = jnp.where(right, X - W + 1, 0)
    for k in range(W):
        store(k, 0, p0 + k)
    for k in range(W - 1):
        store(W + k, 1, q0 + k)
    for k in range(W - 1):
        store(2 * W - 1 + k, 2, q0 + k)


def pack_first(p, q, m, ya, yb, xb):
    even = is_even("gy")
    low = iota((8, Z), 0) < 4
    top, bottom = slice(Y - 8, Y), slice(0, 8)
    for t, (a, b) in enumerate(y_pairs()):
        up = jnp.where(low, pltpu.roll(load(p, q, m, *a, top), 4, 0), load(p, q, m, *b, top))
        down = jnp.where(low, load(p, q, m, *a, bottom), pltpu.roll(load(p, q, m, *b, bottom), 4, 0))
        ya[t] = jnp.where(even, up, down)
        yb[t] = jnp.where(even, down, up)

    def store(k, arr, x):
        xb[k] = load(p, q, m, arr, x)

    face(p, q, m, jnp.logical_not(is_even("gx")), store)


def pack_z(p, q, m, ra, rb, za, zb, yh):
    even = is_even("gy")
    low = iota((8, Z), 0) < 4
    keep_b = b_is_inside("gy")
    for t, (a, b) in enumerate(y_pairs()):
        va = ra[t]
        vb = jnp.where(keep_b, rb[t], 0.0)
        right, left = jnp.where(even, va, vb), jnp.where(even, vb, va)
        yh[a[0] * X + a[1]] = jnp.where(low, right, pltpu.roll(left, 4, 0))
        yh[b[0] * X + b[1]] = jnp.where(low, pltpu.roll(right, 4, 0), left)
    even_z = is_even("gz")
    for r in range(Y // 8 + 1):
        slot = iota((8, Z), 1) // 4
        for tile in range(2):
            up = jnp.zeros((8, Z), F32)
            down = jnp.zeros((8, Z), F32)
            for s in range(32):
                i = tile * 32 + s
                if i >= 3 * X:
                    break
                if r < Y // 8:
                    v = load(p, q, m, i // X, i % X, slice(8 * r, 8 * r + 8))
                else:
                    v = yh[i]
                v = pltpu.roll(v, 4 * s, 1) if s else v
                up = jnp.where(slot == (s + 31) % 32, v, up)
                down = jnp.where(slot == s, v, down)
            za[tile, 8 * r : 8 * r + 8, :] = jnp.where(even_z, up, down)
            zb[tile, 8 * r : 8 * r + 8, :] = jnp.where(even_z, down, up)


ROWS = Y + 8


def pack_x(p, q, m, yh, ra, rb, xa, xbc, zh):
    even = is_even("gz")
    keep_b = b_is_inside("gz")
    lane = iota((ROWS, Z), 1)
    for tile in range(2):
        va = ra[tile]
        vb = jnp.where(keep_b, rb[tile], 0.0)
        right, left = jnp.where(even, va, vb), jnp.where(even, vb, va)
        for s in range(32):
            i = tile * 32 + s
            if i >= 3 * X:
                break
            v = jnp.where(lane // 4 == s, right, left)
            zh[i] = pltpu.roll(v, (Z - 4 * s) % Z, 1) if s else v
    even_x = is_even("gx")
    slot = iota((ROWS, Z), 1) // 8
    main = N_FACE * Y

    def corners(right, out, base):
        acc = [jnp.zeros((ROWS, Z), F32)]

        def store(k, arr, x):
            out[base + 8 * k : base + 8 * k + 8, :] = yh[arr * X + x]
            acc[0] = jnp.where(slot == k, pltpu.roll(zh[arr * X + x], 8 * k + 4, 1), acc[0])

        face(p, q, m, right, store)
        out[base + 8 * N_FACE : base + 8 * N_FACE + ROWS, :] = acc[0]

    corners(jnp.logical_not(even_x), xbc, 0)

    def store(k, arr, x):
        xa[Y * k : Y * k + Y, :] = load(p, q, m, arr, x)

    face(p, q, m, even_x, store)
    corners(even_x, xa, main)


def advance(now, old, gain, put, lo, hi):
    n = X + 2 * W

    def body(j, carry):
        x = lax.rem(j + (lo + n), n)
        xm, xp = lax.rem(x + n - 1, n), lax.rem(x + 1, n)
        c = now[x]
        total = now[xm] + now[xp]
        total = total + pltpu.roll(c, 1, 0) + pltpu.roll(c, ROWS - 1, 0)
        total = total + pltpu.roll(c, 1, 1) + pltpu.roll(c, 2 * Z - 1, 1)
        put(x, (total * (1.0 / 3.0) - old[x]) * gain[x])
        return carry

    lax.fori_loop(0, hi - lo, body, 0)


def run_steps(p, q, m, yh, zh, xbm, xbc, xa, dz, dy, pressure, coef, cur, old, gain):
    ext = (cur, old, gain)
    for arr in range(3):
        for x in range(X):
            ext[arr][x, :Y, :Z] = load(p, q, m, arr, x)
            ext[arr][x, Y:, :Z] = yh[arr * X + x]
            ext[arr][x, :, Z:] = zh[arr * X + x]
    even = is_even("gx")
    keep_b = b_is_inside("gx")

    def unpack(right, main, corner, base, fix):
        z_tile = fix(corner[base + 8 * N_FACE : base + 8 * N_FACE + ROWS, :])
        p0 = jnp.where(right, X, X + W)
        q0 = jnp.where(right, X, X + W + 1)
        for k in range(N_FACE):
            arr = 0 if k < W else 1 if k < 2 * W - 1 else 2
            x = p0 + k if arr == 0 else q0 + (k - W if arr == 1 else k - 2 * W + 1)
            ext[arr][x, :Y, :Z] = fix(main(k))
            ext[arr][x, Y:, :Z] = fix(corner[base + 8 * k : base + 8 * k + 8, :])
            ext[arr][x, :, Z:] = pltpu.roll(z_tile, Z - 8 * k - 4, 1)

    unpack(even, lambda k: xa[Y * k : Y * k + Y, :], xa, N_FACE * Y, lambda v: v)
    unpack(jnp.logical_not(even), lambda k: xbm[k], xbc, 0, lambda v: jnp.where(keep_b, v, 0.0))

    for step in range(ITERS):
        now, before = (cur, old) if step % 2 == 0 else (old, cur)
        reach = ITERS - 1 - step

        def put(x, v, before=before):
            before[x] = v

        advance(now, before, gain, put, -reach, X + reach)
    final = cur if ITERS % 2 == 0 else old
    rows = dct_rows()
    parts = []
    for b in range(X // 8):
        f = [final[8 * b + i, :Y, :Z] for i in range(8)]
        for i in range(8):
            pressure[8 * b + i] = f[i]
        plus = [f[i] + f[7 - i] for i in range(4)]
        minus = [f[i] - f[7 - i] for i in range(4)]
        for k in range(4):
            terms = plus if k % 2 == 0 else minus
            parts.append(sum(float(rows[k, i]) * terms[i] for i in range(4)))
    half = X // 4
    left = jnp.concatenate(parts[:half], axis=0)
    right = jnp.concatenate(parts[half:], axis=0)
    both = jnp.concatenate([left, right], axis=1)
    along_z = jnp.dot(both, dz[...], precision=lax.Precision.HIGHEST, preferred_element_type=F32)
    result = jnp.dot(dy[...], along_z, precision=lax.Precision.HIGHEST, preferred_element_type=F32)
    for d in range(coef.shape[0]):
        coef[d] = result


def place(writer, got, out):
    mine = writer[0, 0] == lax.axis_index("gz")
    low = iota((Y // 2, Z), 1) < Z // 2

    @pl.when(mine)
    def _():
        for t in range(got.shape[0] // 2):
            for h in range(X // 4):
                a = got[2 * t, h * (Y // 2) : (h + 1) * (Y // 2), :]
                b = got[2 * t + 1, h * (Y // 2) : (h + 1) * (Y // 2), :]
                out[0, h, :, t * Z : (t + 1) * Z] = jnp.where(low, a, pltpu.roll(b, Z // 2, 1))
                out[0, h + X // 4, :, t * Z : (t + 1) * Z] = jnp.where(low, pltpu.roll(a, Z // 2, 1), b)

    @pl.when(jnp.logical_not(mine))
    def _():
        out[...] = jnp.zeros_like(out)


def call(kernel, outs, *args, smem=0, scratch=(), limit=40 << 20):
    vm = pl.BlockSpec(memory_space=pltpu.VMEM)
    sm = pl.BlockSpec(memory_space=pltpu.SMEM)
    return pl.pallas_call(
        kernel,
        out_shape=[jax.ShapeDtypeStruct(s, F32) for s in outs],
        in_specs=[sm] * smem + [vm] * (len(args) - smem),
        out_specs=[vm] * len(outs),
        scratch_shapes=list(scratch),
        compiler_params=pltpu.CompilerParams(vmem_limit_bytes=limit),
    )(*args)


def matrices():
    rows = dct_rows()
    z = np.kron(np.eye(Z // 8), rows.T)
    dz = np.kron(np.eye(2), z)
    y = np.kron(np.eye(Y // 8), rows)
    dy = np.kron(np.eye(X // 4), y)
    return dz.astype(np.float32), dy.astype(np.float32)


def per_device(p, q, m, writer):
    sizes = {a: lax.axis_size(a) for a in ("gx", "gy", "gz")}

    def swap(v, axis, kind):
        return lax.ppermute(v, axis, kind(sizes[axis]))

    n_y = X + X // 2
    ya, yb, xb = call(pack_first, [(n_y, 8, Z), (n_y, 8, Z), (N_FACE, Y, Z)], p, q, m)
    ya, yb = swap(ya, "gy", swap_a), swap(yb, "gy", swap_b)
    xb = swap(xb, "gx", swap_b)
    za, zb, yh = call(pack_z, [(2, ROWS, Z), (2, ROWS, Z), (3 * X, 8, Z)], p, q, m, ya, yb)
    za, zb = swap(za, "gz", swap_a), swap(zb, "gz", swap_b)
    n_corner = 8 * N_FACE + ROWS
    xa, xbc, zh = call(
        pack_x, [(N_FACE * Y + n_corner, Z), (n_corner, Z), (3 * X, ROWS, Z)], p, q, m, yh, za, zb
    )
    xa, xbc = swap(xa, "gx", swap_a), swap(xbc, "gx", swap_b)
    dz, dy = matrices()
    ext = pltpu.VMEM((X + 2 * W, ROWS, 2 * Z), F32)
    n = sizes["gz"]
    pressure, coef = call(
        run_steps, [(X, Y, Z), (n, 2 * Y, Z)], p, q, m, yh, zh, xb, xbc, xa, dz, dy, scratch=[ext, ext, ext]
    )
    got = lax.all_to_all(coef, "gz", 0, 0, tiled=True)
    (out,) = call(place, [(1, X // 2, Y // 2, n * Z // 2)], writer, got, smem=1)
    return pressure, out


def solution(mesh):
    return jax.shard_map(
        per_device,
        mesh=mesh,
        in_specs=(P("gx", "gy", "gz"), P("gx", "gy", "gz"), P("gx", "gy", "gz"), P("gx", "gy")),
        out_specs=(P("gx", "gy", "gz"), P("gz", "gx", "gy", None)),
        check_vma=False,
    )
```

```python
import functools

import jax
import jax.numpy as jnp
import numpy as np
from jax import lax
from jax.experimental import pallas as pl
from jax.experimental.pallas import tpu as pltpu
from jax.sharding import PartitionSpec as P

ITERS = 4
X, Y, Z = 16, 64, 128
W = ITERS
N_FACE = W + 2 * (W - 1)
F32 = jnp.float32


def swap_a(v, axis):
    return lax.ppermute(v, axis, [(i, i ^ 1) for i in range(lax.axis_size(axis))])


def swap_b(v, axis):
    other = "gy" if axis == "gx" else "gx"
    names = ("gx", "gy") if axis == "gx" else ("gx", axis)
    n, m = lax.axis_size(axis), lax.axis_size(other)

    def flat(i, o):
        return i * m + o if axis == "gx" else o * n + i

    pairs = []
    for o in range(m):
        for i in range(n):
            j = i + 1 if i % 2 else i - 1
            pairs.append((flat(i, o), flat(j, o) if 0 <= j < n else flat(i, o ^ 1)))
    return lax.ppermute(v, names, pairs)


def dct_rows():
    k = np.arange(4)[:, None]
    i = np.arange(8)[None, :]
    scale = np.where(k == 0, np.sqrt(1.0 / 8.0), np.sqrt(2.0 / 8.0))
    return scale * np.cos(np.pi * (2 * i + 1) * k / 16.0)


def is_even(axis):
    return lax.rem(lax.axis_index(axis), 2) == 0


def b_is_inside(axis):
    index, count = lax.axis_index(axis), lax.axis_size(axis)
    return jnp.logical_and(index > 0, index < count - 1)


def iota(shape, dim):
    return lax.broadcasted_iota(jnp.int32, shape, dim)


def gain_of(mask):
    return 1.0 - 0.5 * mask.astype(F32)


def load(p, q, m, arr, x, rows=slice(None)):
    if arr == 0:
        return p[x, rows, :]
    if arr == 1:
        return q[x, rows, :]
    return gain_of(m[x, rows, :])


def y_pairs():
    return [((0, x), (1, x)) for x in range(X)] + [((2, 2 * i), (2, 2 * i + 1)) for i in range(X // 2)]


def face_items(right):
    p0 = jnp.where(right, X - W, 0)
    q0 = jnp.where(right, X - W + 1, 0)
    return [(0, p0 + k) for k in range(W)] + [(a, q0 + k) for a in (1, 2) for k in range(W - 1)]


def halo_slots(right):
    p0 = jnp.where(right, X + W, 0)
    q0 = jnp.where(right, X + W, 1)
    return [(0, p0 + k) for k in range(W)] + [(a, q0 + k) for a in (1, 2) for k in range(W - 1)]


def pack_y(p, q, m, ya, yb, ep, eq, em, sems):
    copies = []
    for src, dst in ((p, ep), (q, eq), (m, em)):
        for side, at in enumerate((0, Y - 8)):
            copies.append(pltpu.make_async_copy(src.at[:, at : at + 8, :], dst.at[side], sems.at[len(copies)]))
    for c in copies:
        c.start()
    for c in copies:
        c.wait()
    even = is_even("gy")
    low = iota((8, Z), 0) < 4

    def edge(arr, x, side):
        v = (ep, eq, em)[arr][side, x]
        return gain_of(v) if arr == 2 else v

    for t, (a, b) in enumerate(y_pairs()):
        up = jnp.where(low, pltpu.roll(edge(*a, 1), 4, 0), edge(*b, 1))
        down = jnp.where(low, edge(*a, 0), pltpu.roll(edge(*b, 0), 4, 0))
        ya[t] = jnp.where(even, up, down)
        yb[t] = jnp.where(even, down, up)


def pack_faces(p, q, m, _, xa, xb):
    even = is_even("gx")
    for out, right in ((xa, even), (xb, jnp.logical_not(even))):
        for k, (arr, x) in enumerate(face_items(right)):
            out[k] = load(p, q, m, arr, x)


def pack_z(p, q, m, ra, rb, za, zb, yh):
    even = is_even("gy")
    low = iota((8, Z), 0) < 4
    keep_b = b_is_inside("gy")
    for t, (a, b) in enumerate(y_pairs()):
        va = ra[t]
        vb = jnp.where(keep_b, rb[t], 0.0)
        right, left = jnp.where(even, va, vb), jnp.where(even, vb, va)
        yh[a[0] * X + a[1]] = jnp.where(low, right, pltpu.roll(left, 4, 0))
        yh[b[0] * X + b[1]] = jnp.where(low, pltpu.roll(right, 4, 0), left)
    even_z = is_even("gz")
    for r in range(Y // 8 + 1):
        slot = iota((8, Z), 1) // 4
        for tile in range(2):
            up = jnp.zeros((8, Z), F32)
            down = jnp.zeros((8, Z), F32)
            for s in range(32):
                i = tile * 32 + s
                if i >= 3 * X:
                    break
                if r < Y // 8:
                    v = load(p, q, m, i // X, i % X, slice(8 * r, 8 * r + 8))
                else:
                    v = yh[i]
                v = pltpu.roll(v, 4 * s, 1) if s else v
                up = jnp.where(slot == (s + 31) % 32, v, up)
                down = jnp.where(slot == s, v, down)
            za[tile, 8 * r : 8 * r + 8, :] = jnp.where(even_z, up, down)
            zb[tile, 8 * r : 8 * r + 8, :] = jnp.where(even_z, down, up)


ROWS = Y + 2 * W
SLOTS = X + 2 * W
TOP = 8
TALL = TOP + ROWS + 8
CORNER = 8 * N_FACE + ROWS


def z_sides(ra, rb, tile):
    even = is_even("gz")
    va = ra[tile]
    vb = jnp.where(b_is_inside("gz"), rb[tile], 0.0)
    return jnp.where(even, va, vb), jnp.where(even, vb, va)


def z_item(right, left, lane, s):
    v = jnp.where(lane // 4 == s, right, left)
    return pltpu.roll(v, (Z - 4 * s) % Z, 1) if s else v


def pack_x(yh, ra, rb, xac, xbc, zh):
    lane = iota((ROWS, Z), 1)
    edge = set(range(W)) | set(range(X - W, X))
    for tile in range(2):
        right, left = z_sides(ra, rb, tile)
        for s in range(32):
            i = tile * 32 + s
            if i < 3 * X and i % X in edge:
                zh[i] = z_item(right, left, lane, s)
    even_x = is_even("gx")
    slot = lane // 8

    def corners(right, out):
        acc = jnp.zeros((ROWS, Z), F32)
        for k, (arr, x) in enumerate(face_items(right)):
            out[8 * k : 8 * k + 8, :] = yh[arr * X + x]
            acc = jnp.where(slot == k, pltpu.roll(zh[arr * X + x], 8 * k + 4, 1), acc)
        out[8 * N_FACE : CORNER, :] = acc

    corners(jnp.logical_not(even_x), xbc)
    corners(even_x, xac)


def put_rows(ref, s, v):
    ref[s, TOP + W : TOP + W + Y, :] = v[:Y]
    put_edges(ref, s, v[Y:])


def put_edges(ref, s, v):
    ref[s, TOP + W + Y : TOP + ROWS, :] = v[:W]
    ref[s, TOP : TOP + W, :] = v[W:]


def update(out, now, old, gain, s, halo):
    size = 24
    first = iota((size, Z), 1) == 0
    last = iota((size, Z), 1) == Z - 1
    for r in range(TOP, TOP + ROWS, size):
        here, above, below = slice(r, r + size), slice(r - 1, r + size - 1), slice(r + 1, r + size + 1)
        c, h = now[0][s, here, :], now[1][s, here, :]
        cr, hr = pltpu.roll(c, 1, 1), pltpu.roll(h, 1, 1)
        cl, hl = pltpu.roll(c, Z - 1, 1), pltpu.roll(h, Z - 1, 1)
        along_z = (
            jnp.where(first, hr, cr) + jnp.where(last, hl, cl),
            jnp.where(first, cr, hr) + jnp.where(last, cl, hl),
        )
        for i in range(2 if halo else 1):
            total = now[i][s - 1, here, :] + now[i][s + 1, here, :]
            total = total + now[i][s, above, :] + now[i][s, below, :] + along_z[i]
            out[i][s, here, :] = (total * (1.0 / 3.0) - old[i][s, here, :]) * gain[i][s, here, :]


def unflatten(refs):
    pairs = [(refs[2 * i], refs[2 * i + 1]) for i in range(2 + ITERS)] + [(refs[2 * (2 + ITERS)],)]
    return pairs[0], pairs[1], pairs[2:]


N_EXT = 2 * (2 + ITERS) + 1


def run_inside(p, q, m, yh, ra, rb, *refs):
    old, gain, level = unflatten(refs)
    ext = (level[0], old, gain)
    lane = iota((ROWS, Z), 1)
    for tile in range(2):
        right, left = z_sides(ra, rb, tile)
        for s in range(32):
            i = tile * 32 + s
            if i < 3 * X:
                put_rows(ext[i // X][1], W + i % X, z_item(right, left, lane, s))
    for arr in range(3):
        for x in range(X):
            ext[arr][0][W + x, TOP + W : TOP + W + Y, :] = load(p, q, m, arr, x)
            put_edges(ext[arr][0], W + x, yh[arr * X + x])
    for t in range(1, ITERS + 1):
        before = level[t - 2] if t >= 2 else old

        def body(j, carry, t=t, before=before):
            update(level[t], level[t - 1], before, gain, W + t + j, t < ITERS)
            return carry

        lax.fori_loop(0, X - 2 * t, body, 0)


def run_rest(*args):
    xam, xbm, xac, xbc, dz, dy = args[N_EXT : N_EXT + 6]
    refs = args[N_EXT + 6 : 2 * N_EXT + 6]
    pressure, coef = args[2 * N_EXT + 6 :]
    old, gain, level = unflatten(refs)
    ext = (level[0], old, gain)
    even = is_even("gx")
    keep_b = b_is_inside("gx")

    def unpack(right, main, corner, fix):
        z_tile = fix(corner[8 * N_FACE : CORNER, :])
        for k, (arr, s) in enumerate(halo_slots(right)):
            ext[arr][0][s, TOP + W : TOP + W + Y, :] = fix(main[k])
            put_edges(ext[arr][0], s, fix(corner[8 * k : 8 * k + 8, :]))
            put_rows(ext[arr][1], s, pltpu.roll(z_tile, Z - 8 * k - 4, 1))

    unpack(even, xam, xac, lambda v: v)
    unpack(jnp.logical_not(even), xbm, xbc, lambda v: jnp.where(keep_b, v, 0.0))
    for t in range(1, ITERS + 1):
        before = level[t - 2] if t >= 2 else old

        def body(j, carry, t=t, before=before):
            s = jnp.where(j < W, t + j, X + W - t + j - W)
            update(level[t], level[t - 1], before, gain, s, t < ITERS)
            return carry

        lax.fori_loop(0, 2 * W, body, 0)
    rows = dct_rows()
    parts = []
    for b in range(X // 8):
        f = [level[ITERS][0][W + 8 * b + i, TOP + W : TOP + W + Y, :] for i in range(8)]
        for i in range(8):
            pressure[8 * b + i] = f[i]
        plus = [f[i] + f[7 - i] for i in range(4)]
        minus = [f[i] - f[7 - i] for i in range(4)]
        for k in range(4):
            terms = plus if k % 2 == 0 else minus
            parts.append(sum(float(rows[k, i]) * terms[i] for i in range(4)))
    half = X // 4
    left = jnp.concatenate(parts[:half], axis=0)
    right = jnp.concatenate(parts[half:], axis=0)
    both = jnp.concatenate([left, right], axis=1)
    along_z = jnp.dot(both, dz[...], precision=lax.Precision.HIGHEST, preferred_element_type=F32)
    result = jnp.dot(dy[...], along_z, precision=lax.Precision.HIGHEST, preferred_element_type=F32)
    for d in range(coef.shape[0]):
        coef[d] = result


def place(writer, got, out):
    mine = writer[0, 0] == lax.axis_index("gz")
    low = iota((Y // 2, Z), 1) < Z // 2

    @pl.when(mine)
    def _():
        for t in range(got.shape[0] // 2):
            for h in range(X // 4):
                a = got[2 * t, h * (Y // 2) : (h + 1) * (Y // 2), :]
                b = got[2 * t + 1, h * (Y // 2) : (h + 1) * (Y // 2), :]
                out[0, h, :, t * Z : (t + 1) * Z] = jnp.where(low, a, pltpu.roll(b, Z // 2, 1))
                out[0, h + X // 4, :, t * Z : (t + 1) * Z] = jnp.where(low, pltpu.roll(a, Z // 2, 1), b)

    @pl.when(jnp.logical_not(mine))
    def _():
        out[...] = jnp.zeros_like(out)


def call(kernel, outs, *args, first=pltpu.VMEM, n_first=0, scratch=(), aliases=None, cost=1 << 18, flops=0):
    vm = pl.BlockSpec(memory_space=pltpu.VMEM)
    other = pl.BlockSpec(memory_space=first)
    return pl.pallas_call(
        kernel,
        out_shape=[jax.ShapeDtypeStruct(s, F32) for s in outs],
        in_specs=[other] * n_first + [vm] * (len(args) - n_first),
        out_specs=[vm] * len(outs),
        scratch_shapes=list(scratch),
        input_output_aliases=aliases or {},
        cost_estimate=pl.CostEstimate(flops=flops, transcendentals=0, bytes_accessed=cost),
        compiler_params=pltpu.CompilerParams(vmem_limit_bytes=8 << 20),
    )(*args)


def matrices():
    rows = dct_rows()
    z = np.kron(np.eye(Z // 8), rows.T)
    dz = np.kron(np.eye(2), z)
    y = np.kron(np.eye(Y // 8), rows)
    dy = np.kron(np.eye(X // 4), y)
    return dz.astype(np.float32), dy.astype(np.float32)


def per_device(p, q, m, writer):
    n_y = X + X // 2
    edges = [pltpu.VMEM((2, X, 8, Z), d) for d in (F32, F32, jnp.int32)]
    far = [pltpu.with_memory_space_constraint(v, pltpu.HBM) for v in (p, q, m)]
    ya, yb = call(
        pack_y, [(n_y, 8, Z), (n_y, 8, Z)], *far, first=pltpu.HBM, n_first=3,
        scratch=[*edges, pltpu.SemaphoreType.DMA((6,))],
    )
    ya0 = ya
    ya, yb = swap_a(ya, "gy"), swap_b(yb, "gy")
    xa, xb = call(pack_faces, [(N_FACE, Y, Z)] * 2, p, q, m, ya0)
    xa, xb = swap_a(xa, "gx"), swap_b(xb, "gx")
    za, zb, yh = call(pack_z, [(2, ROWS, Z), (2, ROWS, Z), (3 * X, 8, Z)], p, q, m, ya, yb, flops=10000000000)
    za, zb = swap_a(za, "gz"), swap_b(zb, "gz")
    xac, xbc = call(
        pack_x, [(CORNER, Z), (CORNER, Z)], yh, za, zb, scratch=[pltpu.VMEM((3 * X, ROWS, Z), F32)], flops=10000000000
    )
    xac, xbc = swap_a(xac, "gx"), swap_b(xbc, "gx")
    ext = call(run_inside, [(SLOTS, TALL, Z)] * N_EXT, p, q, m, yh, za, zb, flops=10000000000)
    dz, dy = matrices()
    n = lax.axis_size("gz")
    *_, pressure, coef = call(
        run_rest, [(SLOTS, TALL, Z)] * N_EXT + [(X, Y, Z), (n, 2 * Y, Z)], *ext, xa, xb, xac, xbc, dz, dy,
        aliases={i: i for i in range(N_EXT)}, cost=8 << 20,
    )
    got = lax.all_to_all(coef, "gz", 0, 0, tiled=True)
    (out,) = call(place, [(1, X // 2, Y // 2, n * Z // 2)], writer, got, first=pltpu.SMEM, n_first=1)
    return pressure, out


def solution(mesh):
    return jax.shard_map(
        per_device,
        mesh=mesh,
        in_specs=(P("gx", "gy", "gz"), P("gx", "gy", "gz"), P("gx", "gy", "gz"), P("gx", "gy")),
        out_specs=(P("gx", "gy", "gz"), P("gz", "gx", "gy", None)),
        check_vma=False,
    )
```

```python
import functools

import jax
import jax.numpy as jnp
import numpy as np
from jax import lax
from jax.experimental import pallas as pl
from jax.experimental.pallas import tpu as pltpu
from jax.sharding import PartitionSpec as P

ITERS = 4
X, Y, Z = 16, 64, 128
W = ITERS
N_FACE = W + 2 * (W - 1)
F32 = jnp.float32


def swap_a(v, axis):
    return lax.ppermute(v, axis, [(i, i ^ 1) for i in range(lax.axis_size(axis))])


def swap_b(v, axis):
    other = "gy" if axis == "gx" else "gx"
    names = ("gx", "gy") if axis == "gx" else ("gx", axis)
    n, m = lax.axis_size(axis), lax.axis_size(other)

    def flat(i, o):
        return i * m + o if axis == "gx" else o * n + i

    pairs = []
    for o in range(m):
        for i in range(n):
            j = i + 1 if i % 2 else i - 1
            pairs.append((flat(i, o), flat(j, o) if 0 <= j < n else flat(i, o ^ 1)))
    return lax.ppermute(v, names, pairs)


FLOPS_Z, FLOPS_X, FLOPS_IN = 10**9, 10**9, 10**10


def dct_rows():
    k = np.arange(4)[:, None]
    i = np.arange(8)[None, :]
    scale = np.where(k == 0, np.sqrt(1.0 / 8.0), np.sqrt(2.0 / 8.0))
    return scale * np.cos(np.pi * (2 * i + 1) * k / 16.0)


def is_even(axis):
    return lax.rem(lax.axis_index(axis), 2) == 0


def b_is_inside(axis):
    index, count = lax.axis_index(axis), lax.axis_size(axis)
    return jnp.logical_and(index > 0, index < count - 1)


def iota(shape, dim):
    return lax.broadcasted_iota(jnp.int32, shape, dim)


def gain_of(mask):
    return 1.0 - 0.5 * mask.astype(F32)


def load(p, q, m, arr, x, rows=slice(None)):
    if arr == 0:
        return p[x, rows, :]
    if arr == 1:
        return q[x, rows, :]
    return gain_of(m[x, rows, :])


def y_pairs():
    return [((0, x), (1, x)) for x in range(X)] + [((2, 2 * i), (2, 2 * i + 1)) for i in range(X // 2)]


def face_items(right):
    p0 = jnp.where(right, X - W, 0)
    q0 = jnp.where(right, X - W + 1, 0)
    return [(0, p0 + k) for k in range(W)] + [(a, q0 + k) for a in (1, 2) for k in range(W - 1)]


def halo_slots(right):
    p0 = jnp.where(right, X + W, 0)
    q0 = jnp.where(right, X + W, 1)
    return [(0, p0 + k) for k in range(W)] + [(a, q0 + k) for a in (1, 2) for k in range(W - 1)]


def pack_y(p, q, m, ya, yb, ep, eq, em, sems):
    copies = []
    for src, dst in ((p, ep), (q, eq), (m, em)):
        for side, at in enumerate((0, Y - 8)):
            copies.append(pltpu.make_async_copy(src.at[:, at : at + 8, :], dst.at[side], sems.at[len(copies)]))
    for c in copies:
        c.start()
    for c in copies:
        c.wait()
    even = is_even("gy")
    low = iota((8, Z), 0) < 4

    def edge(arr, x, side):
        v = (ep, eq, em)[arr][side, x]
        return gain_of(v) if arr == 2 else v

    for t, (a, b) in enumerate(y_pairs()):
        up = jnp.where(low, pltpu.roll(edge(*a, 1), 4, 0), edge(*b, 1))
        down = jnp.where(low, edge(*a, 0), pltpu.roll(edge(*b, 0), 4, 0))
        ya[t] = jnp.where(even, up, down)
        yb[t] = jnp.where(even, down, up)


def pack_face(lo, hi, p, q, m, _, xb):
    for k, (arr, x) in enumerate(face_items(jnp.logical_not(is_even("gx")))[lo:hi]):
        xb[k] = load(p, q, m, arr, x)


def pack_face_last(writer, p, q, m, _, xb, mine):
    pack_face(CUT, N_FACE, p, q, m, _, xb)
    mine[...] = jnp.full(mine.shape, (writer[0, 0] == lax.axis_index("gz")).astype(F32))


def pack_z(p, q, m, ra, rb, za, zb, yh):
    even = is_even("gy")
    low = iota((8, Z), 0) < 4
    keep_b = b_is_inside("gy")
    for t, (a, b) in enumerate(y_pairs()):
        va = ra[t]
        vb = jnp.where(keep_b, rb[t], 0.0)
        right, left = jnp.where(even, va, vb), jnp.where(even, vb, va)
        yh[a[0] * X + a[1]] = jnp.where(low, right, pltpu.roll(left, 4, 0))
        yh[b[0] * X + b[1]] = jnp.where(low, pltpu.roll(right, 4, 0), left)
    even_z = is_even("gz")
    for r in range(Y // 8 + 1):
        slot = iota((8, Z), 1) // 4
        for tile in range(2):
            up = jnp.zeros((8, Z), F32)
            down = jnp.zeros((8, Z), F32)
            for s in range(32):
                i = tile * 32 + s
                if i >= 3 * X:
                    break
                if r < Y // 8:
                    v = load(p, q, m, i // X, i % X, slice(8 * r, 8 * r + 8))
                else:
                    v = yh[i]
                v = pltpu.roll(v, 4 * s, 1) if s else v
                up = jnp.where(slot == (s + 31) % 32, v, up)
                down = jnp.where(slot == s, v, down)
            za[tile, 8 * r : 8 * r + 8, :] = jnp.where(even_z, up, down)
            zb[tile, 8 * r : 8 * r + 8, :] = jnp.where(even_z, down, up)


ROWS = Y + 2 * W
SLOTS = X + 2 * W
TOP = 8
TALL = TOP + ROWS + 8
CORNER = 8 * N_FACE + ROWS
MAIN = N_FACE * Y
CUT = N_FACE // 2


def z_sides(ra, rb, tile):
    even = is_even("gz")
    va = ra[tile]
    vb = jnp.where(b_is_inside("gz"), rb[tile], 0.0)
    return jnp.where(even, va, vb), jnp.where(even, vb, va)


def z_item(right, left, lane, s):
    v = jnp.where(lane // 4 == s, right, left)
    return pltpu.roll(v, (Z - 4 * s) % Z, 1) if s else v


def pack_x(p, q, m, yh, ra, rb, _, xa, xbc, zh):
    lane = iota((ROWS, Z), 1)
    edge = set(range(W)) | set(range(X - W, X))
    for tile in range(2):
        right, left = z_sides(ra, rb, tile)
        for s in range(32):
            i = tile * 32 + s
            if i < 3 * X and i % X in edge:
                zh[i] = z_item(right, left, lane, s)
    even_x = is_even("gx")
    slot = lane // 8

    def corners(right, out, base):
        acc = jnp.zeros((ROWS, Z), F32)
        for k, (arr, x) in enumerate(face_items(right)):
            out[base + 8 * k : base + 8 * k + 8, :] = yh[arr * X + x]
            acc = jnp.where(slot == k, pltpu.roll(zh[arr * X + x], 8 * k + 4, 1), acc)
        out[base + 8 * N_FACE : base + CORNER, :] = acc

    corners(jnp.logical_not(even_x), xbc, 0)
    corners(even_x, xa, MAIN)
    for k, (arr, x) in enumerate(face_items(even_x)):
        xa[Y * k : Y * k + Y, :] = load(p, q, m, arr, x)


def put_rows(ref, s, v):
    ref[s, TOP + W : TOP + W + Y, :] = v[:Y]
    put_edges(ref, s, v[Y:])


def put_edges(ref, s, v):
    ref[s, TOP + W + Y : TOP + ROWS, :] = v[:W]
    ref[s, TOP : TOP + W, :] = v[W:]


def update(out, now, old, gain, s, last_step):
    size = 32 if last_step else 24
    first = iota((size, Z), 1) == 0
    last = iota((size, Z), 1) == Z - 1
    start, count = (TOP + W, Y) if last_step else (TOP, ROWS)
    for r in range(start, start + count, size):
        here, above, below = slice(r, r + size), slice(r - 1, r + size - 1), slice(r + 1, r + size + 1)
        c, h = now[0][s, here, :], now[1][s, here, :]
        cr, hr = pltpu.roll(c, 1, 1), pltpu.roll(h, 1, 1)
        cl, hl = pltpu.roll(c, Z - 1, 1), pltpu.roll(h, Z - 1, 1)
        along_z = (
            jnp.where(first, hr, cr) + jnp.where(last, hl, cl),
            jnp.where(first, cr, hr) + jnp.where(last, cl, hl),
        )
        for i in range(1 if last_step else 2):
            total = now[i][s - 1, here, :] + now[i][s + 1, here, :]
            total = total + now[i][s, above, :] + now[i][s, below, :] + along_z[i]
            v = (total * (1.0 / 3.0) - old[i][s, here, :]) * gain[i][s, here, :]
            if last_step:
                out[0][s - W, r - start : r - start + size, :] = v
            else:
                out[i][s, here, :] = v


def unflatten(refs):
    pairs = [(refs[2 * i], refs[2 * i + 1]) for i in range(2 + ITERS)] + [(refs[2 * (2 + ITERS)],)]
    return pairs[0], pairs[1], pairs[2:]


N_EXT = 2 * (2 + ITERS) + 1
EXT = [(SLOTS, TALL, Z)] * (N_EXT - 1) + [(X, Y, Z)]


def unpack_face(ext, lo, hi, xb):
    keep_b = b_is_inside("gx")
    for k, (arr, s) in enumerate(halo_slots(jnp.logical_not(is_even("gx")))[lo:hi]):
        ext[arr][0][s, TOP + W : TOP + W + Y, :] = jnp.where(keep_b, xb[k], 0.0)


def run_inside(p, q, m, yh, ra, rb, xb1, *refs):
    old, gain, level = unflatten(refs)
    ext = (level[0], old, gain)
    lane = iota((ROWS, Z), 1)
    for tile in range(2):
        right, left = z_sides(ra, rb, tile)
        for s in range(32):
            i = tile * 32 + s
            if i < 3 * X:
                put_rows(ext[i // X][1], W + i % X, z_item(right, left, lane, s))
    for arr in range(3):
        for x in range(X):
            ext[arr][0][W + x, TOP + W : TOP + W + Y, :] = load(p, q, m, arr, x)
            put_edges(ext[arr][0], W + x, yh[arr * X + x])
    unpack_face(ext, 0, CUT, xb1)
    for t in range(1, ITERS + 1):
        before = level[t - 2] if t >= 2 else old

        def body(j, carry, t=t, before=before):
            update(level[t], level[t - 1], before, gain, W + t + j, t == ITERS)
            return carry

        lax.fori_loop(0, X - 2 * t, body, 0, unroll=True)


def run_rest(*args):
    xb2, xa, xbc, dz, dy = args[N_EXT : N_EXT + 5]
    refs = args[N_EXT + 5 : 2 * N_EXT + 5]
    coef, pressure, sem = args[2 * N_EXT + 5 :]
    old, gain, level = unflatten(refs)
    ext = (level[0], old, gain)
    even = is_even("gx")
    keep_b = b_is_inside("gx")

    def unpack(right, corner, base, fix):
        z_tile = fix(corner[base + 8 * N_FACE : base + CORNER, :])
        for k, (arr, s) in enumerate(halo_slots(right)):
            put_edges(ext[arr][0], s, fix(corner[base + 8 * k : base + 8 * k + 8, :]))
            put_rows(ext[arr][1], s, pltpu.roll(z_tile, Z - 8 * k - 4, 1))

    for k, (arr, s) in enumerate(halo_slots(even)):
        ext[arr][0][s, TOP + W : TOP + W + Y, :] = xa[Y * k : Y * k + Y, :]
    unpack(even, xa, MAIN, lambda v: v)
    unpack_face(ext, CUT, N_FACE, xb2)
    unpack(jnp.logical_not(even), xbc, 0, lambda v: jnp.where(keep_b, v, 0.0))
    for t in range(1, ITERS + 1):
        before = level[t - 2] if t >= 2 else old
        for s in [*range(t, t + W), *range(X + W - t, X + 2 * W - t)]:
            update(level[t], level[t - 1], before, gain, s, t == ITERS)
    final = level[ITERS][0]
    copy = pltpu.make_async_copy(final, pressure, sem)
    copy.start()
    rows = dct_rows()
    parts = []
    for b in range(X // 8):
        f = [final[8 * b + i] for i in range(8)]
        plus = [f[i] + f[7 - i] for i in range(4)]
        minus = [f[i] - f[7 - i] for i in range(4)]
        for k in range(4):
            terms = plus if k % 2 == 0 else minus
            parts.append(sum(float(rows[k, i]) * terms[i] for i in range(4)))
    half = X // 4
    left = jnp.concatenate(parts[:half], axis=0)
    right = jnp.concatenate(parts[half:], axis=0)
    both = jnp.concatenate([left, right], axis=1)
    along_z = jnp.dot(both, dz[...], precision=lax.Precision.HIGHEST, preferred_element_type=F32)
    coef[...] = jnp.dot(dy[...], along_z, precision=lax.Precision.HIGHEST, preferred_element_type=F32)
    copy.wait()


def place(mine, got, out):
    half, rows = X // 4, Y // 2
    low = iota((rows, Z), 1) < Z // 2
    keep = jnp.concatenate([mine[...]] * (rows // 8), axis=0) > 0.5
    for t in range(got.shape[0] // 2):
        for h in range(half):
            a = got[2 * t, h * rows : (h + 1) * rows, :]
            b = got[2 * t + 1, h * rows : (h + 1) * rows, :]
            at = slice(t * Z, (t + 1) * Z)
            out[0, h, :, at] = jnp.where(keep, jnp.where(low, a, pltpu.roll(b, Z // 2, 1)), 0.0)
            out[0, h + half, :, at] = jnp.where(keep, jnp.where(low, pltpu.roll(a, Z // 2, 1), b), 0.0)


def call(kernel, outs, *args, first=pltpu.VMEM, n_first=0, n_far=0, scratch=(), aliases=None, cost=1 << 18, flops=0):
    vm = pl.BlockSpec(memory_space=pltpu.VMEM)
    far = pl.BlockSpec(memory_space=pltpu.HBM)
    other = pl.BlockSpec(memory_space=first)
    return pl.pallas_call(
        kernel,
        out_shape=[jax.ShapeDtypeStruct(s, F32) for s in outs],
        in_specs=[other] * n_first + [vm] * (len(args) - n_first),
        out_specs=[vm] * (len(outs) - n_far) + [far] * n_far,
        scratch_shapes=list(scratch),
        input_output_aliases=aliases or {},
        cost_estimate=pl.CostEstimate(flops=flops, transcendentals=0, bytes_accessed=cost),
        compiler_params=pltpu.CompilerParams(vmem_limit_bytes=8 << 20),
    )(*args)


def matrices():
    rows = dct_rows()
    z = np.kron(np.eye(Z // 8), rows.T)
    dz = np.kron(np.eye(2), z)
    y = np.kron(np.eye(Y // 8), rows)
    dy = np.kron(np.eye(X // 4), y)
    return dz.astype(np.float32), dy.astype(np.float32)


def per_device(p, q, m, writer):
    n_y = X + X // 2
    edges = [pltpu.VMEM((2, X, 8, Z), d) for d in (F32, F32, jnp.int32)]
    far = [pltpu.with_memory_space_constraint(v, pltpu.HBM) for v in (p, q, m)]
    ya, yb = call(
        pack_y, [(n_y, 8, Z), (n_y, 8, Z)], *far, first=pltpu.HBM, n_first=3,
        scratch=[*edges, pltpu.SemaphoreType.DMA((6,))],
    )
    (xb1,) = call(functools.partial(pack_face, 0, CUT), [(CUT, Y, Z)], p, q, m, ya)
    ya, yb = swap_a(ya, "gy"), swap_b(yb, "gy")
    xb1 = swap_b(xb1, "gx")
    za, zb, yh = call(
        pack_z, [(2, ROWS, Z), (2, ROWS, Z), (3 * X, 8, Z)], p, q, m, ya, yb, flops=FLOPS_Z
    )
    xb2, mine = call(
        pack_face_last, [(N_FACE - CUT, Y, Z), (8, Z)], writer, p, q, m, yh, first=pltpu.SMEM, n_first=1
    )
    za, zb = swap_a(za, "gz"), swap_b(zb, "gz")
    xb2 = swap_b(xb2, "gx")
    xa, xbc = call(
        pack_x, [(MAIN + CORNER, Z), (CORNER, Z)], p, q, m, yh, za, zb, xb1, flops=FLOPS_X,
        scratch=[pltpu.VMEM((3 * X, ROWS, Z), F32)],
    )
    xa, xbc = swap_a(xa, "gx"), swap_b(xbc, "gx")
    ext = call(run_inside, EXT, p, q, m, yh, za, zb, xb1, flops=FLOPS_IN)
    dz, dy = matrices()
    n = lax.axis_size("gz")
    *_, coef, pressure = call(
        run_rest, [*EXT, (2 * Y, Z), (X, Y, Z)], *ext, xb2, xa, xbc, dz, dy,
        aliases={i: i for i in range(N_EXT)}, cost=8 << 20, n_far=1, scratch=[pltpu.SemaphoreType.DMA],
    )
    got = lax.all_to_all(jnp.broadcast_to(coef, (n, 2 * Y, Z)), "gz", 0, 0, tiled=True)
    (out,) = call(place, [(1, X // 2, Y // 2, n * Z // 2)], mine, got)
    return pressure, out


def solution(mesh):
    return jax.shard_map(
        per_device,
        mesh=mesh,
        in_specs=(P("gx", "gy", "gz"), P("gx", "gy", "gz"), P("gx", "gy", "gz"), P("gx", "gy")),
        out_specs=(P("gx", "gy", "gz"), P("gz", "gx", "gy", None)),
        check_vma=False,
    )
```

```python
import functools

import jax
import jax.numpy as jnp
import numpy as np
from jax import lax
from jax.experimental import pallas as pl
from jax.experimental.pallas import tpu as pltpu
from jax.sharding import PartitionSpec as P

ITERS = 4
X, Y, Z = 16, 64, 128
W = ITERS
N_FACE = W + 2 * (W - 1)
F32 = jnp.float32


def swap_a(v, axis):
    return lax.ppermute(v, axis, [(i, i ^ 1) for i in range(lax.axis_size(axis))])


def swap_b(v, axis):
    other = "gy" if axis == "gx" else "gx"
    names = ("gx", "gy") if axis == "gx" else ("gx", axis)
    n, m = lax.axis_size(axis), lax.axis_size(other)

    def flat(i, o):
        return i * m + o if axis == "gx" else o * n + i

    pairs = []
    for o in range(m):
        for i in range(n):
            j = i + 1 if i % 2 else i - 1
            pairs.append((flat(i, o), flat(j, o) if 0 <= j < n else flat(i, o ^ 1)))
    return lax.ppermute(v, names, pairs)


FLOPS_Z, FLOPS_X, FLOPS_IN = 10**9, 10**9, 10**10


def dct_rows():
    k = np.arange(4)[:, None]
    i = np.arange(8)[None, :]
    scale = np.where(k == 0, np.sqrt(1.0 / 8.0), np.sqrt(2.0 / 8.0))
    return scale * np.cos(np.pi * (2 * i + 1) * k / 16.0)


def is_even(axis):
    return lax.rem(lax.axis_index(axis), 2) == 0


def b_is_inside(axis):
    index, count = lax.axis_index(axis), lax.axis_size(axis)
    return jnp.logical_and(index > 0, index < count - 1)


def iota(shape, dim):
    return lax.broadcasted_iota(jnp.int32, shape, dim)


def gain_of(mask):
    return 1.0 - 0.5 * mask.astype(F32)


def load(p, q, m, arr, x, rows=slice(None)):
    if arr == 0:
        return p[x, rows, :]
    if arr == 1:
        return q[x, rows, :]
    return gain_of(m[x, rows, :])


def y_pairs():
    return [((0, x), (1, x)) for x in range(X)] + [((2, 2 * i), (2, 2 * i + 1)) for i in range(X // 2)]


def face_items(right):
    p0 = jnp.where(right, X - W, 0)
    q0 = jnp.where(right, X - W + 1, 0)
    return [(0, p0 + k) for k in range(W)] + [(a, q0 + k) for a in (1, 2) for k in range(W - 1)]


def far_items(right):
    p0 = jnp.where(right, X - W + 1, 0)
    q0 = jnp.where(right, X - W + 2, 0)
    return [(0, p0 + k) for k in range(W - 1)] + [(a, q0 + k) for a in (1, 2) for k in range(W - 2)]


def far_slots(right):
    p0 = jnp.where(right, X + W, 1)
    q0 = jnp.where(right, X + W, 2)
    return [(0, p0 + k) for k in range(W - 1)] + [(a, q0 + k) for a in (1, 2) for k in range(W - 2)]


def halo_slots(right):
    p0 = jnp.where(right, X + W, 0)
    q0 = jnp.where(right, X + W, 1)
    return [(0, p0 + k) for k in range(W)] + [(a, q0 + k) for a in (1, 2) for k in range(W - 1)]


def pack_y(p, q, m, ya, yb, ep, eq, em, sems):
    copies = []
    for src, dst in ((p, ep), (q, eq), (m, em)):
        for side, at in enumerate((0, Y - 8)):
            copies.append(pltpu.make_async_copy(src.at[:, at : at + 8, :], dst.at[side], sems.at[len(copies)]))
    for c in copies:
        c.start()
    for c in copies:
        c.wait()
    even = is_even("gy")
    low = iota((8, Z), 0) < 4

    def edge(arr, x, side):
        v = (ep, eq, em)[arr][side, x]
        return gain_of(v) if arr == 2 else v

    for t, (a, b) in enumerate(y_pairs()):
        up = jnp.where(low, pltpu.roll(edge(*a, 1), 4, 0), edge(*b, 1))
        down = jnp.where(low, edge(*a, 0), pltpu.roll(edge(*b, 0), 4, 0))
        ya[t] = jnp.where(even, up, down)
        yb[t] = jnp.where(even, down, up)


def pack_far(p, q, m, _, xb):
    for k, (arr, x) in enumerate(far_items(jnp.logical_not(is_even("gx")))):
        xb[k] = load(p, q, m, arr, x)


def read_writer(writer, _, mine):
    mine[...] = jnp.full(mine.shape, (writer[0, 0] == lax.axis_index("gz")).astype(F32))


def pack_z(p, q, m, ra, rb, za, zb, yh):
    even = is_even("gy")
    low = iota((8, Z), 0) < 4
    keep_b = b_is_inside("gy")
    for t, (a, b) in enumerate(y_pairs()):
        va = ra[t]
        vb = jnp.where(keep_b, rb[t], 0.0)
        right, left = jnp.where(even, va, vb), jnp.where(even, vb, va)
        yh[a[0] * X + a[1]] = jnp.where(low, right, pltpu.roll(left, 4, 0))
        yh[b[0] * X + b[1]] = jnp.where(low, pltpu.roll(right, 4, 0), left)
    even_z = is_even("gz")
    for r in range(Y // 8 + 1):
        slot = iota((8, Z), 1) // 4
        for tile in range(2):
            up = jnp.zeros((8, Z), F32)
            down = jnp.zeros((8, Z), F32)
            for s in range(32):
                i = tile * 32 + s
                if i >= 3 * X:
                    break
                if r < Y // 8:
                    v = load(p, q, m, i // X, i % X, slice(8 * r, 8 * r + 8))
                else:
                    v = yh[i]
                v = pltpu.roll(v, 4 * s, 1) if s else v
                up = jnp.where(slot == (s + 31) % 32, v, up)
                down = jnp.where(slot == s, v, down)
            za[tile, 8 * r : 8 * r + 8, :] = jnp.where(even_z, up, down)
            zb[tile, 8 * r : 8 * r + 8, :] = jnp.where(even_z, down, up)


ROWS = Y + 2 * W
SLOTS = X + 2 * W
TOP = 8
TALL = TOP + ROWS + 8
MAIN = N_FACE * Y
NEAR_ALL = MAIN + 8 * N_FACE + ROWS
N_FAR = 3 * W - 5
FAR_LATE = Y + 8 * N_FAR + ROWS


def z_sides(ra, rb, tile):
    even = is_even("gz")
    va = ra[tile]
    vb = jnp.where(b_is_inside("gz"), rb[tile], 0.0)
    return jnp.where(even, va, vb), jnp.where(even, vb, va)


def z_item(right, left, lane, s):
    v = jnp.where(lane // 4 == s, right, left)
    return pltpu.roll(v, (Z - 4 * s) % Z, 1) if s else v


def next_layer(p, q, m, yh, zh, x):
    c, t, h = p[x], yh[x], zh[x][:Y]
    row, lane = iota((Y, Z), 0), iota((Y, Z), 1)
    total = p[x - 1] + p[x + 1]
    total = total + jnp.where(row == 0, t[7:8], pltpu.roll(c, 1, 0)) + jnp.where(row == Y - 1, t[0:1], pltpu.roll(c, Y - 1, 0))
    total = total + jnp.where(lane == 0, pltpu.roll(h, 1, 1), pltpu.roll(c, 1, 1))
    total = total + jnp.where(lane == Z - 1, pltpu.roll(h, Z - 1, 1), pltpu.roll(c, Z - 1, 1))
    return (total * (1.0 / 3.0) - q[x]) * gain_of(m[x])


def pack_x(p, q, m, yh, ra, rb, _, __, xa, xb, zh):
    lane = iota((ROWS, Z), 1)
    edge = set(range(W)) | set(range(X - W, X))
    for tile in range(2):
        right, left = z_sides(ra, rb, tile)
        for s in range(32):
            i = tile * 32 + s
            if i < 3 * X and i % X in edge:
                zh[i] = z_item(right, left, lane, s)
    even_x = is_even("gx")
    slot = lane // 8

    def corners(items, out, base):
        acc = jnp.zeros((ROWS, Z), F32)
        for k, (arr, x) in enumerate(items):
            out[base + 8 * k : base + 8 * k + 8, :] = yh[arr * X + x]
            acc = jnp.where(slot == k, pltpu.roll(zh[arr * X + x], 8 * k + 4, 1), acc)
        end = base + 8 * len(items)
        out[end : end + ROWS, :] = acc

    xb[:Y, :] = next_layer(p, q, m, yh, zh, jnp.where(even_x, W - 2, X - W + 1))
    corners(far_items(jnp.logical_not(even_x)), xb, Y)
    corners(face_items(even_x), xa, MAIN)
    for k, (arr, x) in enumerate(face_items(even_x)):
        xa[Y * k : Y * k + Y, :] = load(p, q, m, arr, x)


def put_rows(ref, s, v):
    ref[s, TOP + W : TOP + W + Y, :] = v[:Y]
    put_edges(ref, s, v[Y:])


def put_edges(ref, s, v):
    ref[s, TOP + W + Y : TOP + ROWS, :] = v[:W]
    ref[s, TOP : TOP + W, :] = v[W:]


def update(out, now, old, gain, s, last_step):
    size = 32 if last_step else 24
    first = iota((size, Z), 1) == 0
    last = iota((size, Z), 1) == Z - 1
    start, count = (TOP + W, Y) if last_step else (TOP, ROWS)
    for r in range(start, start + count, size):
        here, above, below = slice(r, r + size), slice(r - 1, r + size - 1), slice(r + 1, r + size + 1)
        c, h = now[0][s, here, :], now[1][s, here, :]
        cr, hr = pltpu.roll(c, 1, 1), pltpu.roll(h, 1, 1)
        cl, hl = pltpu.roll(c, Z - 1, 1), pltpu.roll(h, Z - 1, 1)
        along_z = (
            jnp.where(first, hr, cr) + jnp.where(last, hl, cl),
            jnp.where(first, cr, hr) + jnp.where(last, cl, hl),
        )
        for i in range(1 if last_step else 2):
            total = now[i][s - 1, here, :] + now[i][s + 1, here, :]
            total = total + now[i][s, above, :] + now[i][s, below, :] + along_z[i]
            v = (total * (1.0 / 3.0) - old[i][s, here, :]) * gain[i][s, here, :]
            if last_step:
                out[0][s - W, r - start : r - start + size, :] = v
            else:
                out[i][s, here, :] = v


def unflatten(refs):
    pairs = [(refs[2 * i], refs[2 * i + 1]) for i in range(2 + ITERS)] + [(refs[2 * (2 + ITERS)],)]
    return pairs[0], pairs[1], pairs[2:]


N_EXT = 2 * (2 + ITERS) + 1
EXT = [(SLOTS, TALL, Z)] * (N_EXT - 1) + [(X, Y, Z)]


def run_inside(p, q, m, yh, ra, rb, xf, *refs):
    old, gain, level = unflatten(refs)
    ext = (level[0], old, gain)
    lane = iota((ROWS, Z), 1)
    for tile in range(2):
        right, left = z_sides(ra, rb, tile)
        for s in range(32):
            i = tile * 32 + s
            if i < 3 * X:
                put_rows(ext[i // X][1], W + i % X, z_item(right, left, lane, s))
    for arr in range(3):
        for x in range(X):
            ext[arr][0][W + x, TOP + W : TOP + W + Y, :] = load(p, q, m, arr, x)
            put_edges(ext[arr][0], W + x, yh[arr * X + x])
    keep_b = b_is_inside("gx")
    for k, (arr, s) in enumerate(far_slots(jnp.logical_not(is_even("gx")))):
        ext[arr][0][s, TOP + W : TOP + W + Y, :] = jnp.where(keep_b, xf[k], 0.0)
    for t in range(1, ITERS + 1):
        before = level[t - 2] if t >= 2 else old

        def body(j, carry, t=t, before=before):
            update(level[t], level[t - 1], before, gain, W + t + j, t == ITERS)
            return carry

        lax.fori_loop(0, X - 2 * t, body, 0, unroll=True)


def unpack_corners(ext, slots, corner, base, fix):
    end = base + 8 * len(slots)
    z_tile = fix(corner[end : end + ROWS, :])
    for k, (arr, s) in enumerate(slots):
        put_edges(ext[arr][0], s, fix(corner[base + 8 * k : base + 8 * k + 8, :]))
        put_rows(ext[arr][1], s, pltpu.roll(z_tile, Z - 8 * k - 4, 1))


def run_side(right, old, gain, level, first_count):
    for t in range(1, ITERS + 1):
        before = level[t - 2] if t >= 2 else old
        for j in range(first_count if t == 1 else W):
            s = jnp.where(right, X + W - t + j, W + t - 1 - j)
            update(level[t], level[t - 1], before, gain, s, t == ITERS)


def run_near(*args):
    xa = args[N_EXT]
    old, gain, level = unflatten(args[N_EXT + 1 :])
    ext = (level[0], old, gain)
    even = is_even("gx")
    slots = halo_slots(even)
    for k, (arr, s) in enumerate(slots):
        ext[arr][0][s, TOP + W : TOP + W + Y, :] = xa[Y * k : Y * k + Y, :]
    unpack_corners(ext, slots, xa, MAIN, lambda v: v)
    run_side(even, old, gain, level, W)


def run_far(*args):
    xb, dz, dy = args[N_EXT : N_EXT + 3]
    refs = args[N_EXT + 3 : 2 * N_EXT + 3]
    coef, pressure, sem = args[2 * N_EXT + 3 :]
    old, gain, level = unflatten(refs)
    ext = (level[0], old, gain)
    right = jnp.logical_not(is_even("gx"))
    keep_b = b_is_inside("gx")

    def fix(v):
        return jnp.where(keep_b, v, 0.0)

    unpack_corners(ext, far_slots(right), xb, Y, fix)
    level[1][0][jnp.where(right, X + 2 * W - 2, 1), TOP + W : TOP + W + Y, :] = fix(xb[:Y, :])
    run_side(right, old, gain, level, W - 1)
    final = level[ITERS][0]
    copy = pltpu.make_async_copy(final, pressure, sem)
    copy.start()
    rows = dct_rows()
    parts = []
    for b in range(X // 8):
        f = [final[8 * b + i] for i in range(8)]
        plus = [f[i] + f[7 - i] for i in range(4)]
        minus = [f[i] - f[7 - i] for i in range(4)]
        for k in range(4):
            terms = plus if k % 2 == 0 else minus
            parts.append(sum(float(rows[k, i]) * terms[i] for i in range(4)))
    half = X // 4
    left = jnp.concatenate(parts[:half], axis=0)
    right = jnp.concatenate(parts[half:], axis=0)
    both = jnp.concatenate([left, right], axis=1)
    along_z = jnp.dot(both, dz[...], precision=lax.Precision.HIGHEST, preferred_element_type=F32)
    coef[...] = jnp.dot(dy[...], along_z, precision=lax.Precision.HIGHEST, preferred_element_type=F32)
    copy.wait()


def place(mine, got, out, buf, sems):
    half, rows = X // 4, Y // 2
    low = iota((rows, Z), 1) < Z // 2
    keep = jnp.concatenate([mine[...]] * (rows // 8), axis=0) > 0.5
    copies = []
    for h in range(half):
        for t in range(got.shape[0] // 2):
            a = got[2 * t, h * rows : (h + 1) * rows, :]
            b = got[2 * t + 1, h * rows : (h + 1) * rows, :]
            at = slice(t * Z, (t + 1) * Z)
            buf[h, :, at] = jnp.where(keep, jnp.where(low, a, pltpu.roll(b, Z // 2, 1)), 0.0)
            buf[h + half, :, at] = jnp.where(keep, jnp.where(low, pltpu.roll(a, Z // 2, 1), b), 0.0)
        for i in (h, h + half):
            copies.append(pltpu.make_async_copy(buf.at[i], out.at[0, i], sems.at[i]))
            copies[-1].start()
    for c in copies:
        c.wait()


def call(kernel, outs, *args, first=pltpu.VMEM, n_first=0, n_far=0, scratch=(), aliases=None, cost=1 << 18, flops=0):
    vm = pl.BlockSpec(memory_space=pltpu.VMEM)
    far = pl.BlockSpec(memory_space=pltpu.HBM)
    other = pl.BlockSpec(memory_space=first)
    return pl.pallas_call(
        kernel,
        out_shape=[jax.ShapeDtypeStruct(s, F32) for s in outs],
        in_specs=[other] * n_first + [vm] * (len(args) - n_first),
        out_specs=[vm] * (len(outs) - n_far) + [far] * n_far,
        scratch_shapes=list(scratch),
        input_output_aliases=aliases or {},
        cost_estimate=pl.CostEstimate(flops=flops, transcendentals=0, bytes_accessed=cost),
        compiler_params=pltpu.CompilerParams(vmem_limit_bytes=8 << 20),
    )(*args)


def matrices():
    rows = dct_rows()
    z = np.kron(np.eye(Z // 8), rows.T)
    dz = np.kron(np.eye(2), z)
    y = np.kron(np.eye(Y // 8), rows)
    dy = np.kron(np.eye(X // 4), y)
    return dz.astype(np.float32), dy.astype(np.float32)


def per_device(p, q, m, writer):
    n_y = X + X // 2
    edges = [pltpu.VMEM((2, X, 8, Z), d) for d in (F32, F32, jnp.int32)]
    far = [pltpu.with_memory_space_constraint(v, pltpu.HBM) for v in (p, q, m)]
    ya, yb = call(
        pack_y, [(n_y, 8, Z), (n_y, 8, Z)], *far, first=pltpu.HBM, n_first=3,
        scratch=[*edges, pltpu.SemaphoreType.DMA((6,))],
    )
    (xf,) = call(pack_far, [(N_FAR, Y, Z)], p, q, m, ya)
    ya, yb = swap_a(ya, "gy"), swap_b(yb, "gy")
    xf = swap_b(xf, "gx")
    za, zb, yh = call(
        pack_z, [(2, ROWS, Z), (2, ROWS, Z), (3 * X, 8, Z)], p, q, m, ya, yb, flops=FLOPS_Z
    )
    za, zb = swap_a(za, "gz"), swap_b(zb, "gz")
    (mine,) = call(read_writer, [(8, Z)], writer, yh, first=pltpu.SMEM, n_first=1)
    xa, xb = call(
        pack_x, [(NEAR_ALL, Z), (FAR_LATE, Z)], p, q, m, yh, za, zb, xf, mine, flops=FLOPS_X,
        scratch=[pltpu.VMEM((3 * X, ROWS, Z), F32)],
    )
    xa, xb = swap_a(xa, "gx"), swap_b(xb, "gx")
    same = {i: i for i in range(N_EXT)}
    ext = call(run_inside, EXT, p, q, m, yh, za, zb, xf, flops=FLOPS_IN)
    ext = call(run_near, EXT, *ext, xa, aliases=same, flops=FLOPS_IN)
    dz, dy = matrices()
    n = lax.axis_size("gz")
    *_, coef, pressure = call(
        run_far, [*EXT, (2 * Y, Z), (X, Y, Z)], *ext, xb, dz, dy,
        aliases=same, n_far=1, scratch=[pltpu.SemaphoreType.DMA],
    )
    got = lax.all_to_all(jnp.broadcast_to(coef, (n, 2 * Y, Z)), "gz", 0, 0, tiled=True)
    size = (X // 2, Y // 2, n * Z // 2)
    (out,) = call(
        place, [(1, *size)], mine, got, n_far=1, scratch=[pltpu.VMEM(size, F32), pltpu.SemaphoreType.DMA((X // 2,))]
    )
    return pressure, out


def solution(mesh):
    return jax.shard_map(
        per_device,
        mesh=mesh,
        in_specs=(P("gx", "gy", "gz"), P("gx", "gy", "gz"), P("gx", "gy", "gz"), P("gx", "gy")),
        out_specs=(P("gx", "gy", "gz"), P("gz", "gx", "gy", None)),
        check_vma=False,
    )
```

```python
import functools

import jax
import jax.numpy as jnp
import numpy as np
from jax import lax
from jax.experimental import pallas as pl
from jax.experimental.pallas import tpu as pltpu
from jax.sharding import PartitionSpec as P

ITERS = 4
X, Y, Z = 16, 64, 128
W = ITERS
N_FACE = W + 2 * (W - 1)
F32 = jnp.float32


def swap_a(v, axis):
    return lax.ppermute(v, axis, [(i, i ^ 1) for i in range(lax.axis_size(axis))])


def swap_b(v, axis):
    other = "gy" if axis == "gx" else "gx"
    names = ("gx", "gy") if axis == "gx" else ("gx", axis)
    n, m = lax.axis_size(axis), lax.axis_size(other)

    def flat(i, o):
        return i * m + o if axis == "gx" else o * n + i

    pairs = []
    for o in range(m):
        for i in range(n):
            j = i + 1 if i % 2 else i - 1
            pairs.append((flat(i, o), flat(j, o) if 0 <= j < n else flat(i, o ^ 1)))
    return lax.ppermute(v, names, pairs)


FLOPS_Z, FLOPS_X, FLOPS_IN = 10**9, 10**9, 10**10


def dct_rows():
    k = np.arange(4)[:, None]
    i = np.arange(8)[None, :]
    scale = np.where(k == 0, np.sqrt(1.0 / 8.0), np.sqrt(2.0 / 8.0))
    return scale * np.cos(np.pi * (2 * i + 1) * k / 16.0)


def is_even(axis):
    return lax.rem(lax.axis_index(axis), 2) == 0


def b_is_inside(axis):
    index, count = lax.axis_index(axis), lax.axis_size(axis)
    return jnp.logical_and(index > 0, index < count - 1)


def iota(shape, dim):
    return lax.broadcasted_iota(jnp.int32, shape, dim)


def gain_of(mask):
    return 1.0 - 0.5 * mask.astype(F32)


def load(p, q, m, arr, x, rows=slice(None)):
    if arr == 0:
        return p[x, rows, :]
    if arr == 1:
        return q[x, rows, :]
    return gain_of(m[x, rows, :])


def y_pairs():
    return [((0, x), (1, x)) for x in range(X)] + [((2, 2 * i), (2, 2 * i + 1)) for i in range(X // 2)]


def face_items(right):
    p0 = jnp.where(right, X - W, 0)
    q0 = jnp.where(right, X - W + 1, 0)
    return [(0, p0 + k) for k in range(W)] + [(a, q0 + k) for a in (1, 2) for k in range(W - 1)]


def far_items(right):
    p0 = jnp.where(right, X - W + 1, 0)
    q0 = jnp.where(right, X - W + 2, 0)
    return [(0, p0 + k) for k in range(W - 1)] + [(a, q0 + k) for a in (1, 2) for k in range(W - 2)]


def halo_items(right, width):
    def at(k, n):
        return jnp.where(right, k, n - 1 - k)

    return [(0, at(k, width)) for k in range(width)] + [(a, at(k, width - 1)) for a in (1, 2) for k in range(width - 1)]


def pack_y(p, q, m, ya, yb, ep, eq, em, sems):
    copies = []
    for src, dst in ((p, ep), (q, eq), (m, em)):
        for side, at in enumerate((0, Y - 8)):
            copies.append(pltpu.make_async_copy(src.at[:, at : at + 8, :], dst.at[side], sems.at[len(copies)]))
    for c in copies:
        c.start()
    for c in copies:
        c.wait()
    even = is_even("gy")
    low = iota((8, Z), 0) < 4

    def edge(arr, x, side):
        v = (ep, eq, em)[arr][side, x]
        return gain_of(v) if arr == 2 else v

    for t, (a, b) in enumerate(y_pairs()):
        up = jnp.where(low, pltpu.roll(edge(*a, 1), 4, 0), edge(*b, 1))
        down = jnp.where(low, edge(*a, 0), pltpu.roll(edge(*b, 0), 4, 0))
        ya[t] = jnp.where(even, up, down)
        yb[t] = jnp.where(even, down, up)


def pack_far(p, q, m, _, xb):
    for k, (arr, x) in enumerate(far_items(jnp.logical_not(is_even("gx")))):
        xb[k] = load(p, q, m, arr, x)


def read_writer(writer, _, mine):
    mine[...] = jnp.full(mine.shape, (writer[0, 0] == lax.axis_index("gz")).astype(F32))


def pack_z(p, q, m, ra, rb, za, zb, yh):
    even = is_even("gy")
    low = iota((8, Z), 0) < 4
    keep_b = b_is_inside("gy")
    for t, (a, b) in enumerate(y_pairs()):
        va = ra[t]
        vb = jnp.where(keep_b, rb[t], 0.0)
        right, left = jnp.where(even, va, vb), jnp.where(even, vb, va)
        yh[a[0] * X + a[1]] = jnp.where(low, right, pltpu.roll(left, 4, 0))
        yh[b[0] * X + b[1]] = jnp.where(low, pltpu.roll(right, 4, 0), left)
    even_z = is_even("gz")
    for r in range(Y // 8 + 1):
        slot = iota((8, Z), 1) // 4
        for tile in range(2):
            up = jnp.zeros((8, Z), F32)
            down = jnp.zeros((8, Z), F32)
            for s in range(32):
                i = tile * 32 + s
                if i >= 3 * X:
                    break
                if r < Y // 8:
                    v = load(p, q, m, i // X, i % X, slice(8 * r, 8 * r + 8))
                else:
                    v = yh[i]
                v = pltpu.roll(v, 4 * s, 1) if s else v
                up = jnp.where(slot == (s + 31) % 32, v, up)
                down = jnp.where(slot == s, v, down)
            za[tile, 8 * r : 8 * r + 8, :] = jnp.where(even_z, up, down)
            zb[tile, 8 * r : 8 * r + 8, :] = jnp.where(even_z, down, up)


ROWS = Y + 2 * W
TOP = 8
TALL = TOP + ROWS + 8
MAIN = N_FACE * Y
NEAR_ALL = MAIN + 8 * N_FACE + ROWS
N_FAR = 3 * W - 5
FAR_LATE = Y + 8 * N_FAR + ROWS


def z_sides(ra, rb, tile):
    even = is_even("gz")
    va = ra[tile]
    vb = jnp.where(b_is_inside("gz"), rb[tile], 0.0)
    return jnp.where(even, va, vb), jnp.where(even, vb, va)


def z_item(right, left, lane, s):
    v = jnp.where(lane // 4 == s, right, left)
    return pltpu.roll(v, (Z - 4 * s) % Z, 1) if s else v


def next_layer(p, q, m, yh, zh, x):
    c, t, h = p[x], yh[x], zh[x][:Y]
    row, lane = iota((Y, Z), 0), iota((Y, Z), 1)
    total = p[x - 1] + p[x + 1]
    total = total + jnp.where(row == 0, t[7:8], pltpu.roll(c, 1, 0)) + jnp.where(row == Y - 1, t[0:1], pltpu.roll(c, Y - 1, 0))
    total = total + jnp.where(lane == 0, pltpu.roll(h, 1, 1), pltpu.roll(c, 1, 1))
    total = total + jnp.where(lane == Z - 1, pltpu.roll(h, Z - 1, 1), pltpu.roll(c, Z - 1, 1))
    return (total * (1.0 / 3.0) - q[x]) * gain_of(m[x])


def pack_x(p, q, m, yh, rb, ra, _, xa, xb, zh):
    lane = iota((ROWS, Z), 1)
    edge = set(range(W)) | set(range(X - W, X))
    for tile in range(2):
        right, left = z_sides(ra, rb, tile)
        for s in range(32):
            i = tile * 32 + s
            if i < 3 * X and i % X in edge:
                zh[i] = z_item(right, left, lane, s)
    even_x = is_even("gx")
    slot = lane // 8

    def corners(items, out, base):
        acc = jnp.zeros((ROWS, Z), F32)
        for k, (arr, x) in enumerate(items):
            out[base + 8 * k : base + 8 * k + 8, :] = yh[arr * X + x]
            acc = jnp.where(slot == k, pltpu.roll(zh[arr * X + x], 8 * k + 4, 1), acc)
        end = base + 8 * len(items)
        out[end : end + ROWS, :] = acc

    xb[:Y, :] = next_layer(p, q, m, yh, zh, jnp.where(even_x, W - 2, X - W + 1))
    corners(far_items(jnp.logical_not(even_x)), xb, Y)
    corners(face_items(even_x), xa, MAIN)
    for k, (arr, x) in enumerate(face_items(even_x)):
        xa[Y * k : Y * k + Y, :] = load(p, q, m, arr, x)


def put_rows(ref, s, v):
    ref[s, TOP + W : TOP + W + Y, :] = v[:Y]
    put_edges(ref, s, v[Y:])


def put_edges(ref, s, v):
    ref[s, TOP + W + Y : TOP + ROWS, :] = v[:W]
    ref[s, TOP : TOP + W, :] = v[W:]


def views(pair, i):
    return tuple(ref.at[i] for ref in pair)


def update(out, centre, one_side, other_side, old, gain):
    last_step = len(out) == 1
    size = 32 if last_step else 24
    first = iota((size, Z), 1) == 0
    last = iota((size, Z), 1) == Z - 1
    start, count = (TOP + W, Y) if last_step else (TOP, ROWS)
    for r in range(start, start + count, size):
        here, above, below = slice(r, r + size), slice(r - 1, r + size - 1), slice(r + 1, r + size + 1)
        c, h = centre[0][here, :], centre[1][here, :]
        cr, hr = pltpu.roll(c, 1, 1), pltpu.roll(h, 1, 1)
        cl, hl = pltpu.roll(c, Z - 1, 1), pltpu.roll(h, Z - 1, 1)
        along_z = (
            jnp.where(first, hr, cr) + jnp.where(last, hl, cl),
            jnp.where(first, cr, hr) + jnp.where(last, cl, hl),
        )
        for i in range(len(out)):
            total = one_side[i][here, :] + other_side[i][here, :]
            total = total + centre[i][above, :] + centre[i][below, :] + along_z[i]
            v = (total * (1.0 / 3.0) - old[i][here, :]) * gain[i][here, :]
            if last_step:
                out[i][r - start : r - start + size, :] = v
            else:
                out[i][here, :] = v


def pairs(refs):
    return [tuple(refs[i : i + 2]) for i in range(0, len(refs), 2)]


N_EXT = 2 * (2 + ITERS)


def run_inside(p, q, m, yh, rb, ra, *refs):
    (old, gain, *level), inner = pairs(refs[:N_EXT]), refs[N_EXT]
    ext = (level[0], old, gain)
    lane = iota((ROWS, Z), 1)
    for tile in range(2):
        right, left = z_sides(ra, rb, tile)
        for s in range(32):
            i = tile * 32 + s
            if i < 3 * X:
                put_rows(ext[i // X][1], i % X, z_item(right, left, lane, s))
    for arr in range(3):
        for x in range(X):
            ext[arr][0][x, TOP + W : TOP + W + Y, :] = load(p, q, m, arr, x)
            put_edges(ext[arr][0], x, yh[arr * X + x])
    for t in range(1, ITERS + 1):
        before = level[t - 2] if t >= 2 else old
        for x in range(t, X - t):
            out = (inner.at[x - W],) if t == ITERS else views(level[t], x)
            now = [views(level[t - 1], x + d) for d in (0, -1, 1)]
            update(out, *now, views(before, x), views(gain, x))


def halo_scratch(width):
    sizes = [width, width - 1, width - 1] + [W] * (ITERS - 1)
    return [pltpu.VMEM((n, TALL, Z), F32) for n in sizes for _ in range(2)]


N_HALO = 2 * (2 + ITERS)


def unpack_corners(halo, items, corner, base, fix):
    end = base + 8 * len(items)
    z_tile = fix(corner[end : end + ROWS, :])
    for k, (arr, i) in enumerate(items):
        put_edges(halo[arr][0], i, fix(corner[base + 8 * k : base + 8 * k + 8, :]))
        put_rows(halo[arr][1], i, pltpu.roll(z_tile, Z - 8 * k - 4, 1))


def run_side(right, known, halo, final, given):
    old, gain, *level = known
    beyond, strip = halo[:3], halo[2:]

    def own(e):
        return jnp.where(right, X - 1 + e, -e)

    def either(arr, inside, e):
        return views(beyond[arr], e - 1) if e >= 1 else views(inside, own(e))

    def at(t, e):
        if t == 0:
            return either(0, level[0], e)
        return views(strip[t], e + t - 1) if e > -t else views(level[t], own(e))

    for t in range(1, ITERS + 1):
        for e in range(1 - t, W + 1 - t - (given if t == 1 else 0)):
            out = (final.at[jnp.where(right, W - 1 + e, -e)],) if t == ITERS else views(strip[t], e + t - 1)
            before = at(t - 2, e) if t >= 2 else either(1, old, e)
            update(out, at(t - 1, e), at(t - 1, e - 1), at(t - 1, e + 1), before, either(2, gain, e))


def run_near(*args):
    known, xa, final, halo = pairs(args[:N_EXT]), args[N_EXT], args[N_EXT + 1], pairs(args[N_EXT + 2 :])
    even = is_even("gx")
    items = halo_items(even, W)
    for k, (arr, i) in enumerate(items):
        halo[arr][0][i, TOP + W : TOP + W + Y, :] = xa[Y * k : Y * k + Y, :]
    unpack_corners(halo, items, xa, MAIN, lambda v: v)
    run_side(even, known, halo, final, 0)


def run_far(*args):
    known, rest = pairs(args[:N_EXT]), args[N_EXT:]
    inner, near, xf, xb, dz, dy, coef, far = rest[:8]
    halo = pairs(rest[8:])
    even = is_even("gx")
    right = jnp.logical_not(even)
    keep_b = b_is_inside("gx")

    def fix(v):
        return jnp.where(keep_b, v, 0.0)

    items = halo_items(right, W - 1)
    for k, (arr, i) in enumerate(items):
        halo[arr][0][i, TOP + W : TOP + W + Y, :] = fix(xf[k])
    unpack_corners(halo, items, xb, Y, fix)
    halo[3][0][W - 1, TOP + W : TOP + W + Y, :] = fix(xb[:Y, :])
    run_side(right, known, halo, far, 1)
    low = [jnp.where(even, far[i], near[i]) for i in range(W)]
    high = [jnp.where(even, near[i], far[i]) for i in range(W)]
    layers = [*low, *(inner[i] for i in range(X - 2 * W)), *high]
    rows = dct_rows()
    parts = []
    for b in range(X // 8):
        f = layers[8 * b : 8 * b + 8]
        plus = [f[i] + f[7 - i] for i in range(4)]
        minus = [f[i] - f[7 - i] for i in range(4)]
        for k in range(4):
            terms = plus if k % 2 == 0 else minus
            parts.append(sum(float(rows[k, i]) * terms[i] for i in range(4)))
    half = X // 4
    left = jnp.concatenate(parts[:half], axis=0)
    right = jnp.concatenate(parts[half:], axis=0)
    both = jnp.concatenate([left, right], axis=1)
    along_z = jnp.dot(both, dz[...], precision=lax.Precision.HIGHEST, preferred_element_type=F32)
    coef[...] = jnp.dot(dy[...], along_z, precision=lax.Precision.HIGHEST, preferred_element_type=F32)


def place(mine, got, inner, near, far, out, pressure, buf, sems):
    even = is_even("gx")
    near_at, far_at = jnp.where(even, X - W, 0), jnp.where(even, 0, X - W)
    copies = [
        pltpu.make_async_copy(inner, pressure.at[pl.ds(W, X - 2 * W)], sems.at[X // 2]),
        pltpu.make_async_copy(near, pressure.at[pl.ds(near_at, W)], sems.at[X // 2 + 1]),
        pltpu.make_async_copy(far, pressure.at[pl.ds(far_at, W)], sems.at[X // 2 + 2]),
    ]
    for c in copies:
        c.start()
    half, rows = X // 4, Y // 2
    low = iota((rows, Z), 1) < Z // 2
    keep = jnp.concatenate([mine[...]] * (rows // 8), axis=0) > 0.5
    for h in range(half):
        for t in range(got.shape[0] // 2):
            a = got[2 * t, h * rows : (h + 1) * rows, :]
            b = got[2 * t + 1, h * rows : (h + 1) * rows, :]
            at = slice(t * Z, (t + 1) * Z)
            buf[h, :, at] = jnp.where(keep, jnp.where(low, a, pltpu.roll(b, Z // 2, 1)), 0.0)
            buf[h + half, :, at] = jnp.where(keep, jnp.where(low, pltpu.roll(a, Z // 2, 1), b), 0.0)
        for i in (h, h + half):
            copies.append(pltpu.make_async_copy(buf.at[i], out.at[0, i], sems.at[i]))
            copies[-1].start()
    for c in copies:
        c.wait()


def call(kernel, outs, *args, first=pltpu.VMEM, n_first=0, n_far=0, scratch=(), flops=0):
    vm = pl.BlockSpec(memory_space=pltpu.VMEM)
    far = pl.BlockSpec(memory_space=pltpu.HBM)
    other = pl.BlockSpec(memory_space=first)
    return pl.pallas_call(
        kernel,
        out_shape=[jax.ShapeDtypeStruct(s, F32) for s in outs],
        in_specs=[other] * n_first + [vm] * (len(args) - n_first),
        out_specs=[vm] * (len(outs) - n_far) + [far] * n_far,
        scratch_shapes=list(scratch),
        cost_estimate=pl.CostEstimate(flops=flops, transcendentals=0, bytes_accessed=1 << 18),
        compiler_params=pltpu.CompilerParams(vmem_limit_bytes=8 << 20),
    )(*args)


def matrices():
    rows = dct_rows()
    z = np.kron(np.eye(Z // 8), rows.T)
    dz = np.kron(np.eye(2), z)
    y = np.kron(np.eye(Y // 8), rows)
    dy = np.kron(np.eye(X // 4), y)
    return dz.astype(np.float32), dy.astype(np.float32)


def per_device(p, q, m, writer):
    n_y = X + X // 2
    edges = [pltpu.VMEM((2, X, 8, Z), d) for d in (F32, F32, jnp.int32)]
    far = [pltpu.with_memory_space_constraint(v, pltpu.HBM) for v in (p, q, m)]
    ya, yb = call(
        pack_y, [(n_y, 8, Z), (n_y, 8, Z)], *far, first=pltpu.HBM, n_first=3,
        scratch=[*edges, pltpu.SemaphoreType.DMA((6,))],
    )
    ya, yb = swap_a(ya, "gy"), swap_b(yb, "gy")
    za, zb, yh = call(
        pack_z, [(2, ROWS, Z), (2, ROWS, Z), (3 * X, 8, Z)], p, q, m, ya, yb, flops=FLOPS_Z
    )
    za, zb = swap_a(za, "gz"), swap_b(zb, "gz")
    (xf,) = call(pack_far, [(N_FAR, Y, Z)], p, q, m, yh)
    xf = swap_b(xf, "gx")
    (mine,) = call(read_writer, [(8, Z)], writer, yh, first=pltpu.SMEM, n_first=1)
    xa, xb = call(
        pack_x, [(NEAR_ALL, Z), (FAR_LATE, Z)], p, q, m, yh, zb, za, mine, flops=FLOPS_X,
        scratch=[pltpu.VMEM((3 * X, ROWS, Z), F32)],
    )
    xa, xb = swap_a(xa, "gx"), swap_b(xb, "gx")
    *ext, inner = call(
        run_inside, [(X, TALL, Z)] * N_EXT + [(X - 2 * W, Y, Z)], p, q, m, yh, zb, za, flops=FLOPS_IN
    )
    (near,) = call(run_near, [(W, Y, Z)], *ext, xa, scratch=halo_scratch(W))
    dz, dy = matrices()
    n = lax.axis_size("gz")
    coef, far = call(
        run_far, [(2 * Y, Z), (W, Y, Z)], *ext, inner, near, xf, xb, dz, dy, scratch=halo_scratch(W - 1)
    )
    got = lax.all_to_all(jnp.broadcast_to(coef, (n, 2 * Y, Z)), "gz", 0, 0, tiled=True)
    size = (X // 2, Y // 2, n * Z // 2)
    out, pressure = call(
        place, [(1, *size), (X, Y, Z)], mine, got, inner, near, far, n_far=2,
        scratch=[pltpu.VMEM(size, F32), pltpu.SemaphoreType.DMA((X // 2 + 3,))],
    )
    return pressure, out


def solution(mesh):
    return jax.shard_map(
        per_device,
        mesh=mesh,
        in_specs=(P("gx", "gy", "gz"), P("gx", "gy", "gz"), P("gx", "gy", "gz"), P("gx", "gy")),
        out_specs=(P("gx", "gy", "gz"), P("gz", "gx", "gy", None)),
        check_vma=False,
    )
```

```python
import functools

import jax
import jax.numpy as jnp
import numpy as np
from jax import lax
from jax.experimental import pallas as pl
from jax.experimental.pallas import tpu as pltpu
from jax.sharding import PartitionSpec as P

ITERS = 4
X, Y, Z = 16, 64, 128
W = ITERS
N_FACE = W + 2 * (W - 1)
F32 = jnp.float32


def swap_a(v, axis):
    return lax.ppermute(v, axis, [(i, i ^ 1) for i in range(lax.axis_size(axis))])


def swap_b(v, axis):
    other = "gy" if axis == "gx" else "gx"
    names = ("gx", "gy") if axis == "gx" else ("gx", axis)
    n, m = lax.axis_size(axis), lax.axis_size(other)

    def flat(i, o):
        return i * m + o if axis == "gx" else o * n + i

    pairs = []
    for o in range(m):
        for i in range(n):
            j = i + 1 if i % 2 else i - 1
            pairs.append((flat(i, o), flat(j, o) if 0 <= j < n else flat(i, o ^ 1)))
    return lax.ppermute(v, names, pairs)


FLOPS_Z, FLOPS_X, FLOPS_IN = 10**9, 10**9, 10**10
FIRST = 6


def dct_rows():
    k = np.arange(4)[:, None]
    i = np.arange(8)[None, :]
    scale = np.where(k == 0, np.sqrt(1.0 / 8.0), np.sqrt(2.0 / 8.0))
    return scale * np.cos(np.pi * (2 * i + 1) * k / 16.0)


def is_even(axis):
    return lax.rem(lax.axis_index(axis), 2) == 0


def b_is_inside(axis):
    index, count = lax.axis_index(axis), lax.axis_size(axis)
    return jnp.logical_and(index > 0, index < count - 1)


def iota(shape, dim):
    return lax.broadcasted_iota(jnp.int32, shape, dim)


def gain_of(mask):
    return 1.0 - 0.5 * mask.astype(F32)


def load(p, q, m, arr, x, rows=slice(None)):
    if arr == 0:
        return p[x, rows, :]
    if arr == 1:
        return q[x, rows, :]
    return gain_of(m[x, rows, :])


def y_pairs():
    return [((0, x), (1, x)) for x in range(X)] + [((2, 2 * i), (2, 2 * i + 1)) for i in range(X // 2)]


def face_items(right):
    p0 = jnp.where(right, X - W, 0)
    q0 = jnp.where(right, X - W + 1, 0)
    return [(0, p0 + k) for k in range(W)] + [(a, q0 + k) for a in (1, 2) for k in range(W - 1)]


def far_items(right):
    p0 = jnp.where(right, X - W + 1, 0)
    q0 = jnp.where(right, X - W + 2, 0)
    return [(0, p0 + k) for k in range(W - 1)] + [(a, q0 + k) for a in (1, 2) for k in range(W - 2)]


def halo_items(right, width):
    def at(k, n):
        return jnp.where(right, k, n - 1 - k)

    return [(0, at(k, width)) for k in range(width)] + [(a, at(k, width - 1)) for a in (1, 2) for k in range(width - 1)]


def pack_y(p, q, m, ya, yb, ep, eq, em, sems):
    copies = []
    for src, dst in ((p, ep), (q, eq), (m, em)):
        for side, at in enumerate((0, Y - 8)):
            copies.append(pltpu.make_async_copy(src.at[:, at : at + 8, :], dst.at[side], sems.at[len(copies)]))
    for c in copies:
        c.start()
    for c in copies:
        c.wait()
    even = is_even("gy")
    low = iota((8, Z), 0) < 4

    def edge(arr, x, side):
        v = (ep, eq, em)[arr][side, x]
        return gain_of(v) if arr == 2 else v

    for t, (a, b) in enumerate(y_pairs()):
        up = jnp.where(low, pltpu.roll(edge(*a, 1), 4, 0), edge(*b, 1))
        down = jnp.where(low, edge(*a, 0), pltpu.roll(edge(*b, 0), 4, 0))
        ya[t] = jnp.where(even, up, down)
        yb[t] = jnp.where(even, down, up)


def pack_far(p, q, m, _, xb):
    for k, (arr, x) in enumerate(far_items(jnp.logical_not(is_even("gx")))):
        xb[k] = load(p, q, m, arr, x)


def read_writer(writer, _, mine):
    mine[...] = jnp.full(mine.shape, (writer[0, 0] == lax.axis_index("gz")).astype(F32))


def pack_z(p, q, m, ra, rb, za, zb, yh):
    even = is_even("gy")
    low = iota((8, Z), 0) < 4
    keep_b = b_is_inside("gy")
    for t, (a, b) in enumerate(y_pairs()):
        va = ra[t]
        vb = jnp.where(keep_b, rb[t], 0.0)
        right, left = jnp.where(even, va, vb), jnp.where(even, vb, va)
        yh[a[0] * X + a[1]] = jnp.where(low, right, pltpu.roll(left, 4, 0))
        yh[b[0] * X + b[1]] = jnp.where(low, pltpu.roll(right, 4, 0), left)
    even_z = is_even("gz")
    for r in range(Y // 8 + 1):
        slot = iota((8, Z), 1) // 4
        for tile in range(2):
            up = jnp.zeros((8, Z), F32)
            down = jnp.zeros((8, Z), F32)
            for s in range(32):
                i = tile * 32 + s
                if i >= 3 * X:
                    break
                if r < Y // 8:
                    v = load(p, q, m, i // X, i % X, slice(8 * r, 8 * r + 8))
                else:
                    v = yh[i]
                v = pltpu.roll(v, 4 * s, 1) if s else v
                up = jnp.where(slot == (s + 31) % 32, v, up)
                down = jnp.where(slot == s, v, down)
            za[tile, 8 * r : 8 * r + 8, :] = jnp.where(even_z, up, down)
            zb[tile, 8 * r : 8 * r + 8, :] = jnp.where(even_z, down, up)


ROWS = Y + 2 * W
TOP = 8
TALL = TOP + ROWS + 8
MAIN = N_FACE * Y
NEAR_ALL = MAIN + 8 * N_FACE + ROWS
N_FAR = 3 * W - 5
FAR_LATE = Y + 8 * N_FAR + ROWS


def z_sides(ra, rb, tile):
    even = is_even("gz")
    va = ra[tile]
    vb = jnp.where(b_is_inside("gz"), rb[tile], 0.0)
    return jnp.where(even, va, vb), jnp.where(even, vb, va)


def z_item(right, left, lane, s):
    v = jnp.where(lane // 4 == s, right, left)
    return pltpu.roll(v, (Z - 4 * s) % Z, 1) if s else v


def next_layer(p, q, m, yh, zh, x):
    c, t, h = p[x], yh[x], zh[x][:Y]
    row, lane = iota((Y, Z), 0), iota((Y, Z), 1)
    total = p[x - 1] + p[x + 1]
    total = total + jnp.where(row == 0, t[7:8], pltpu.roll(c, 1, 0)) + jnp.where(row == Y - 1, t[0:1], pltpu.roll(c, Y - 1, 0))
    total = total + jnp.where(lane == 0, pltpu.roll(h, 1, 1), pltpu.roll(c, 1, 1))
    total = total + jnp.where(lane == Z - 1, pltpu.roll(h, Z - 1, 1), pltpu.roll(c, Z - 1, 1))
    return (total * (1.0 / 3.0) - q[x]) * gain_of(m[x])


def pack_x(p, q, m, yh, rb, ra, _, xa, xb, zh):
    lane = iota((ROWS, Z), 1)
    edge = set(range(W)) | set(range(X - W, X))
    for tile in range(2):
        right, left = z_sides(ra, rb, tile)
        for s in range(32):
            i = tile * 32 + s
            if i < 3 * X and i % X in edge:
                zh[i] = z_item(right, left, lane, s)
    even_x = is_even("gx")
    slot = lane // 8

    def corners(items, out, base):
        acc = jnp.zeros((ROWS, Z), F32)
        for k, (arr, x) in enumerate(items):
            out[base + 8 * k : base + 8 * k + 8, :] = yh[arr * X + x]
            acc = jnp.where(slot == k, pltpu.roll(zh[arr * X + x], 8 * k + 4, 1), acc)
        end = base + 8 * len(items)
        out[end : end + ROWS, :] = acc

    xb[:Y, :] = next_layer(p, q, m, yh, zh, jnp.where(even_x, W - 2, X - W + 1))
    corners(far_items(jnp.logical_not(even_x)), xb, Y)
    corners(face_items(even_x), xa, MAIN)
    for k, (arr, x) in enumerate(face_items(even_x)):
        xa[Y * k : Y * k + Y, :] = load(p, q, m, arr, x)


def put_rows(ref, s, v):
    ref[s, TOP + W : TOP + W + Y, :] = v[:Y]
    put_edges(ref, s, v[Y:])


def put_edges(ref, s, v):
    ref[s, TOP + W + Y : TOP + ROWS, :] = v[:W]
    ref[s, TOP : TOP + W, :] = v[W:]


def views(pair, i):
    return tuple(ref.at[i] for ref in pair)


def update(out, centre, one_side, other_side, old, gain):
    last_step = len(out) == 1
    size = 32 if last_step else 24
    first = iota((size, Z), 1) == 0
    last = iota((size, Z), 1) == Z - 1
    start, count = (TOP + W, Y) if last_step else (TOP, ROWS)
    for r in range(start, start + count, size):
        here, above, below = slice(r, r + size), slice(r - 1, r + size - 1), slice(r + 1, r + size + 1)
        c, h = centre[0][here, :], centre[1][here, :]
        cr, hr = pltpu.roll(c, 1, 1), pltpu.roll(h, 1, 1)
        cl, hl = pltpu.roll(c, Z - 1, 1), pltpu.roll(h, Z - 1, 1)
        along_z = (
            jnp.where(first, hr, cr) + jnp.where(last, hl, cl),
            jnp.where(first, cr, hr) + jnp.where(last, cl, hl),
        )
        for i in range(len(out)):
            total = one_side[i][here, :] + other_side[i][here, :]
            total = total + centre[i][above, :] + centre[i][below, :] + along_z[i]
            v = (total * (1.0 / 3.0) - old[i][here, :]) * gain[i][here, :]
            if last_step:
                out[i][r - start : r - start + size, :] = v
            else:
                out[i][here, :] = v


def pairs(refs):
    return [tuple(refs[i : i + 2]) for i in range(0, len(refs), 2)]


N_EXT = 2 * (2 + ITERS)


def run_inside(p, q, m, yh, rb, ra, *refs):
    (old, gain, *level), inner = pairs(refs[:N_EXT]), refs[N_EXT]
    ext = (level[0], old, gain)
    lane = iota((ROWS, Z), 1)
    for tile in range(2):
        right, left = z_sides(ra, rb, tile)
        for s in range(32):
            i = tile * 32 + s
            if i < 3 * X:
                put_rows(ext[i // X][1], i % X, z_item(right, left, lane, s))
    for arr in range(3):
        for x in range(X):
            ext[arr][0][x, TOP + W : TOP + W + Y, :] = load(p, q, m, arr, x)
            put_edges(ext[arr][0], x, yh[arr * X + x])
    for t in range(1, ITERS + 1):
        before = level[t - 2] if t >= 2 else old
        for x in range(t, X - t):
            out = (inner.at[x - W],) if t == ITERS else views(level[t], x)
            now = [views(level[t - 1], x + d) for d in (0, -1, 1)]
            update(out, *now, views(before, x), views(gain, x))


def halo_scratch(width):
    sizes = [width, width - 1, width - 1] + [W] * (ITERS - 1)
    return [pltpu.VMEM((n, TALL, Z), F32) for n in sizes for _ in range(2)]


N_HALO = 2 * (2 + ITERS)


def unpack_corners(halo, items, corner, base, fix):
    end = base + 8 * len(items)
    z_tile = fix(corner[end : end + ROWS, :])
    for k, (arr, i) in enumerate(items):
        put_edges(halo[arr][0], i, fix(corner[base + 8 * k : base + 8 * k + 8, :]))
        put_rows(halo[arr][1], i, pltpu.roll(z_tile, Z - 8 * k - 4, 1))


def run_side(right, known, halo, final, given):
    old, gain, *level = known
    beyond, strip = halo[:3], halo[2:]

    def own(e):
        return jnp.where(right, X - 1 + e, -e)

    def either(arr, inside, e):
        return views(beyond[arr], e - 1) if e >= 1 else views(inside, own(e))

    def at(t, e):
        if t == 0:
            return either(0, level[0], e)
        return views(strip[t], e + t - 1) if e > -t else views(level[t], own(e))

    for t in range(1, ITERS + 1):
        for e in range(1 - t, W + 1 - t - (given if t == 1 else 0)):
            out = (final.at[jnp.where(right, W - 1 + e, -e)],) if t == ITERS else views(strip[t], e + t - 1)
            before = at(t - 2, e) if t >= 2 else either(1, old, e)
            update(out, at(t - 1, e), at(t - 1, e - 1), at(t - 1, e + 1), before, either(2, gain, e))


def run_near(*args):
    known, xa, final, halo = pairs(args[:N_EXT]), args[N_EXT], args[N_EXT + 1], pairs(args[N_EXT + 2 :])
    even = is_even("gx")
    items = halo_items(even, W)
    for k, (arr, i) in enumerate(items):
        halo[arr][0][i, TOP + W : TOP + W + Y, :] = xa[Y * k : Y * k + Y, :]
    unpack_corners(halo, items, xa, MAIN, lambda v: v)
    run_side(even, known, halo, final, 0)


def run_far(*args):
    known, rest = pairs(args[:N_EXT]), args[N_EXT:]
    inner, near, xf, xb, dz, dy, coef, far = rest[:8]
    halo = pairs(rest[8:])
    even = is_even("gx")
    right = jnp.logical_not(even)
    keep_b = b_is_inside("gx")

    def fix(v):
        return jnp.where(keep_b, v, 0.0)

    items = halo_items(right, W - 1)
    for k, (arr, i) in enumerate(items):
        halo[arr][0][i, TOP + W : TOP + W + Y, :] = fix(xf[k])
    unpack_corners(halo, items, xb, Y, fix)
    halo[3][0][W - 1, TOP + W : TOP + W + Y, :] = fix(xb[:Y, :])
    run_side(right, known, halo, far, 1)
    low = [jnp.where(even, far[i], near[i]) for i in range(W)]
    high = [jnp.where(even, near[i], far[i]) for i in range(W)]
    layers = [*low, *(inner[i] for i in range(X - 2 * W)), *high]
    rows = dct_rows()
    parts = []
    for b in range(X // 8):
        f = layers[8 * b : 8 * b + 8]
        plus = [f[i] + f[7 - i] for i in range(4)]
        minus = [f[i] - f[7 - i] for i in range(4)]
        for k in range(4):
            terms = plus if k % 2 == 0 else minus
            parts.append(sum(float(rows[k, i]) * terms[i] for i in range(4)))
    half = X // 4
    left = jnp.concatenate(parts[:half], axis=0)
    right = jnp.concatenate(parts[half:], axis=0)
    both = jnp.concatenate([left, right], axis=1)
    along_z = jnp.dot(both, dz[...], precision=lax.Precision.HIGHEST, preferred_element_type=F32)
    coef[...] = jnp.dot(dy[...], along_z, precision=lax.Precision.HIGHEST, preferred_element_type=F32)


def gather_order(place_in_group, n):
    return (place_in_group + FIRST) % n


def place(mine, got, inner, near, far, out, pressure, buf, sems):
    even = is_even("gx")
    near_at, far_at = jnp.where(even, X - W, 0), jnp.where(even, 0, X - W)
    copies = [
        pltpu.make_async_copy(inner, pressure.at[pl.ds(W, X - 2 * W)], sems.at[X // 2]),
        pltpu.make_async_copy(near, pressure.at[pl.ds(near_at, W)], sems.at[X // 2 + 1]),
        pltpu.make_async_copy(far, pressure.at[pl.ds(far_at, W)], sems.at[X // 2 + 2]),
    ]
    for c in copies:
        c.start()
    half, rows = X // 4, Y // 2
    n = got.shape[0]
    source = {gather_order(i, n): i for i in range(n)}
    low = iota((rows, Z), 1) < Z // 2
    keep = jnp.concatenate([mine[...]] * (rows // 8), axis=0) > 0.5
    for h in range(half):
        for t in range(n // 2):
            a = got[source[2 * t], h * rows : (h + 1) * rows, :]
            b = got[source[2 * t + 1], h * rows : (h + 1) * rows, :]
            at = slice(t * Z, (t + 1) * Z)
            buf[h, :, at] = jnp.where(keep, jnp.where(low, a, pltpu.roll(b, Z // 2, 1)), 0.0)
            buf[h + half, :, at] = jnp.where(keep, jnp.where(low, pltpu.roll(a, Z // 2, 1), b), 0.0)
        for i in (h, h + half):
            copies.append(pltpu.make_async_copy(buf.at[i], out.at[0, i], sems.at[i]))
            copies[-1].start()
    for c in copies:
        c.wait()


def call(kernel, outs, *args, first=pltpu.VMEM, n_first=0, n_far=0, scratch=(), flops=0):
    vm = pl.BlockSpec(memory_space=pltpu.VMEM)
    far = pl.BlockSpec(memory_space=pltpu.HBM)
    other = pl.BlockSpec(memory_space=first)
    return pl.pallas_call(
        kernel,
        out_shape=[jax.ShapeDtypeStruct(s, F32) for s in outs],
        in_specs=[other] * n_first + [vm] * (len(args) - n_first),
        out_specs=[vm] * (len(outs) - n_far) + [far] * n_far,
        scratch_shapes=list(scratch),
        cost_estimate=pl.CostEstimate(flops=flops, transcendentals=0, bytes_accessed=1 << 18),
        compiler_params=pltpu.CompilerParams(vmem_limit_bytes=8 << 20),
    )(*args)


def matrices():
    rows = dct_rows()
    z = np.kron(np.eye(Z // 8), rows.T)
    dz = np.kron(np.eye(2), z)
    y = np.kron(np.eye(Y // 8), rows)
    dy = np.kron(np.eye(X // 4), y)
    return dz.astype(np.float32), dy.astype(np.float32)


def per_device(p, q, m, writer):
    n_y = X + X // 2
    edges = [pltpu.VMEM((2, X, 8, Z), d) for d in (F32, F32, jnp.int32)]
    far = [pltpu.with_memory_space_constraint(v, pltpu.HBM) for v in (p, q, m)]
    ya, yb = call(
        pack_y, [(n_y, 8, Z), (n_y, 8, Z)], *far, first=pltpu.HBM, n_first=3,
        scratch=[*edges, pltpu.SemaphoreType.DMA((6,))],
    )
    ya, yb = swap_a(ya, "gy"), swap_b(yb, "gy")
    za, zb, yh = call(
        pack_z, [(2, ROWS, Z), (2, ROWS, Z), (3 * X, 8, Z)], p, q, m, ya, yb, flops=FLOPS_Z
    )
    za, zb = swap_a(za, "gz"), swap_b(zb, "gz")
    (xf,) = call(pack_far, [(N_FAR, Y, Z)], p, q, m, yh)
    xf = swap_b(xf, "gx")
    (mine,) = call(read_writer, [(8, Z)], writer, yh, first=pltpu.SMEM, n_first=1)
    xa, xb = call(
        pack_x, [(NEAR_ALL, Z), (FAR_LATE, Z)], p, q, m, yh, zb, za, mine, flops=FLOPS_X,
        scratch=[pltpu.VMEM((3 * X, ROWS, Z), F32)],
    )
    xa, xb = swap_a(xa, "gx"), swap_b(xb, "gx")
    *ext, inner = call(
        run_inside, [(X, TALL, Z)] * N_EXT + [(X - 2 * W, Y, Z)], p, q, m, yh, zb, za, flops=FLOPS_IN
    )
    (near,) = call(run_near, [(W, Y, Z)], *ext, xa, scratch=halo_scratch(W))
    dz, dy = matrices()
    n = lax.axis_size("gz")
    coef, far = call(
        run_far, [(2 * Y, Z), (W, Y, Z)], *ext, inner, near, xf, xb, dz, dy, scratch=halo_scratch(W - 1)
    )
    group = [gather_order(i, n) for i in range(n)]
    got = lax.all_to_all(
        jnp.broadcast_to(coef, (n, 2 * Y, Z)), "gz", 0, 0, axis_index_groups=[group], tiled=True
    )
    size = (X // 2, Y // 2, n * Z // 2)
    out, pressure = call(
        place, [(1, *size), (X, Y, Z)], mine, got, inner, near, far, n_far=2,
        scratch=[pltpu.VMEM(size, F32), pltpu.SemaphoreType.DMA((X // 2 + 3,))],
    )
    return pressure, out


def solution(mesh):
    return jax.shard_map(
        per_device,
        mesh=mesh,
        in_specs=(P("gx", "gy", "gz"), P("gx", "gy", "gz"), P("gx", "gy", "gz"), P("gx", "gy")),
        out_specs=(P("gx", "gy", "gz"), P("gz", "gx", "gy", None)),
        check_vma=False,
    )
```
